32 devices in a mesh: groups: 2 (over x), rep: 16 (over z, y, core).
Axes of the slice: x: 2, y: 2, z: 4, core: 2. Of those that a mesh axis runs over, the one named last changes fastest.
Arguments:
- queries: bfloat16 [256, 8192], P(('groups', 'rep')), parts along dimension 0, may hold values from -200 to 200
- incoming_pair: bfloat16 [256, 2, 1024], P(('groups', 'rep')), parts along dimension 0, may hold values from -6 to 6
- cache_key_value: bfloat16 [256, 2, 128, 1024], P(('groups', 'rep')), parts along dimension 0, may hold values from -40 to 40
- cache_length: int32 [256], P(('groups', 'rep')), parts along dimension 0, may hold values from 2 to 128, as said below
- out_weight: bfloat16 [8192, 8192], P('rep'), may hold values from -0.0625 to 0.0625
- adapter_down: bfloat16 [64, 8192, 64], P(('groups', 'rep')), parts along dimension 0, may hold values from -0.0625 to 0.0625
- adapter_up: bfloat16 [64, 64, 8192], P(('groups', 'rep')), parts along dimension 0, may hold values from -0.75 to 0.75
- request_adapter: int32 [256], P(('groups', 'rep')), parts along dimension 0, may hold values from 0 to 31
- adapter_slot: int32 [64], P('groups'), parts along dimension 0, may hold values from 0 to 31, each once
Outputs:
- projected: bfloat16 [256, 8192], P(('groups', 'rep')), parts along dimension 0
The draws below stay inside these ranges and needn't reach their ends.
There are 2 independent parts, one for each index of `groups`. The reference program is written for one: setup_inputs(seed, part) draws one part's arguments, and reference() takes and returns one part's arrays. A program takes and returns all parts, laid end to end along the dimension named above; an argument that names none is the same for every part. Nothing has to cross between parts.
Inputs may be any that keep to these rules, and one draw needn't show every extreme that they name: `cache_length`: some request has all 128 slots live. `adapter_slot`: each of the 32 slots once; slot s is stored with index s on dimension 0.
All inputs are finite; a program needn't handle non-finite values.
Results may differ from the reference program's by a relative error of at most 0.007.
Values may be sent and summed in bfloat16 or wider, within the bound.
No kernel may reach another device: no remote copies, remote signals or barrier semaphores. Data moves between devices by JAX's collectives and lax.ppermute only.
A program may use at most 128 MiB of HBM per device.

```python
import math
import jax
import jax.numpy as jnp
import numpy as np
from jax import lax

D = 8192
QUERY_HEADS = 64
KEY_VALUE_HEADS = 8
HEAD_SIZE = 128
RANK = 64
CACHE_SLOTS = 128
REQUEST_COUNT = 128
ADAPTERS = 32


def cache_fields(key, low, high):
    random_noise_key, spread_key, twin_key = jax.random.split(key, 3)
    record_fields = jax.random.normal(random_noise_key, (REQUEST_COUNT, 2, CACHE_SLOTS, KEY_VALUE_HEADS * HEAD_SIZE), jnp.float32)
    spread = jnp.exp(jax.random.uniform(spread_key, (REQUEST_COUNT, 1, CACHE_SLOTS, 1), jnp.float32, math.log(low), math.log(high)))
    key_rows = record_fields[:, 0:1] * spread
    leading = key_rows[:, 0, 0]
    partner = leading + spread[:, 0, 0] * jax.random.normal(twin_key, leading.shape, jnp.float32)
    key_rows = key_rows.at[:, 0, 1].set(partner)
    stacked = jnp.concatenate([key_rows, record_fields[:, 1:2]], axis=1)
    return jnp.clip(stacked, -40.0, 40.0)


def draw_queries(key, part):
    key = jax.random.fold_in(key, 5)
    drawn = jax.random.normal(key, (REQUEST_COUNT, QUERY_HEADS * HEAD_SIZE), jnp.float32)
    return jnp.clip(drawn, -200.0, 200.0).astype(jnp.bfloat16)


def draw_cache_key_value(key, part):
    stacked = cache_fields(key, 0.5, 2.0)
    return stacked.astype(jnp.bfloat16)


def draw_cache_length(key, part):
    key = jax.random.fold_in(key, 7)
    first_key, second_key = jax.random.split(key)
    lengths = jax.random.randint(first_key, (REQUEST_COUNT,), 2, CACHE_SLOTS + 1)
    chosen = jax.random.randint(second_key, (), 0, REQUEST_COUNT)
    return lengths.at[chosen].set(CACHE_SLOTS).astype(jnp.int32)


def with_ends(result, own_key, smallest, high):
    longest = result.shape.index(max(result.shape))
    spots = []
    for shift in (0, 1):
        where = [jax.random.randint(jax.random.fold_in(own_key, axis), (), 0, length) for axis, length in enumerate(result.shape)]
        where[longest] = (where[longest] + shift) % result.shape[longest]
        spots.append(tuple(where))
    return result.at[spots[0]].set(smallest).at[spots[1]].set(high)


def steps_of(own_key, shape, cuts, smallest, top_value):
    gain, own = 1.0, jax.random.fold_in(own_key, 6)
    for axis_at, blocks in cuts:
        draws = jnp.exp(jax.random.uniform(jax.random.fold_in(own, axis_at), (blocks,), jnp.float32, smallest / len(cuts), top_value / len(cuts)))
        gain = gain * jnp.repeat(draws, shape[axis_at] // blocks).reshape([-1 if axis == axis_at else 1 for axis in range(len(shape))])
    return gain


def rank_bounds(amount, slope):
    weights = [(1 << 20) // math.isqrt(standing ** slope) + 1 for standing in range(1, amount + 1)]
    scale = 1 + sum(weights) // (1 << 30)
    return np.cumsum(np.array([max(1, weight // scale) for weight in weights]))


def ranked_ids(stream_key, dims, number_of, skew):
    listing = rank_bounds(number_of, skew)
    ticket = jax.random.randint(jax.random.fold_in(stream_key, 1), dims, 0, int(listing[number_of - 1]))
    rank = jnp.searchsorted(jnp.asarray(listing, jnp.int32), ticket, side="right")
    return jax.random.permutation(jax.random.fold_in(stream_key, 2), number_of)[rank].astype(jnp.int32)


def centred(stream_key, shape, deviation, limit, cuts=(), kind=jnp.bfloat16):
    drawn = deviation * jax.random.normal(stream_key, shape, jnp.float32)
    if cuts:
        drawn = drawn * steps_of(stream_key, shape, cuts, -0.22, 0.18)
    return jnp.clip(drawn, -limit, limit).astype(kind)


def setup_inputs(seed: int = 0, part: int = 0) -> dict:
    key_list = jax.random.split(jax.random.key(seed), 10)
    part_splits = jax.random.split(jax.random.fold_in(key_list[9], part), 10)
    return {
        "queries": draw_queries(jax.random.fold_in(jax.random.fold_in(key_list[9], part), 71), part),
        "incoming_pair": centred(part_splits[1], (REQUEST_COUNT, 2, KEY_VALUE_HEADS * HEAD_SIZE), 1.0, 6.0, ((0, 16),)),
        "cache_key_value": draw_cache_key_value(jax.random.fold_in(jax.random.fold_in(key_list[9], part), 71), part),
        "cache_length": draw_cache_length(jax.random.fold_in(jax.random.fold_in(key_list[9], part), 71), part),
        "out_weight": centred(key_list[4], (D, D), D ** -0.5, 0.0625, ((0, 16),)),
        "adapter_down": centred(part_splits[5], (ADAPTERS, D, RANK), D ** -0.5, 0.0625, ((0, 16),)),
        "adapter_up": centred(part_splits[6], (ADAPTERS, RANK, D), RANK ** -0.5, 0.75, ((0, 16),)),
        "request_adapter": with_ends(ranked_ids(part_splits[7], (REQUEST_COUNT,), ADAPTERS, 2), jax.random.fold_in(part_splits[7], 3), 0, ADAPTERS - 1).astype(jnp.int32),
        "adapter_slot": jax.random.permutation(part_splits[8], ADAPTERS).astype(jnp.int32),
    }


ADAPTER_GAIN = 2.0
MASKED_SCORE = -1e30


def attend(queries, incoming_pair, cache_key_value, cache_length):
    request_batch = queries.shape[0]
    grouped_query = QUERY_HEADS // KEY_VALUE_HEADS
    scaling = HEAD_SIZE ** -0.5
    query_head_rows = queries.astype(jnp.float32).reshape(request_batch, KEY_VALUE_HEADS, grouped_query, HEAD_SIZE)
    cache_key_rows = cache_key_value[:, 0].astype(jnp.float32).reshape(request_batch, CACHE_SLOTS, KEY_VALUE_HEADS, HEAD_SIZE)
    cache_value_rows = cache_key_value[:, 1].astype(jnp.float32).reshape(request_batch, CACHE_SLOTS, KEY_VALUE_HEADS, HEAD_SIZE)
    incoming_key = incoming_pair[:, 0].astype(jnp.float32).reshape(request_batch, KEY_VALUE_HEADS, HEAD_SIZE)
    incoming_value = incoming_pair[:, 1].astype(jnp.float32).reshape(request_batch, KEY_VALUE_HEADS, HEAD_SIZE)
    scores = jnp.einsum("rkgd,rlkd->rkgl", query_head_rows, cache_key_rows) * scaling
    live_slot = jnp.arange(CACHE_SLOTS, dtype=jnp.int32)[None, :] < cache_length[:, None]
    scores = jnp.where(live_slot[:, None, None, :], scores, MASKED_SCORE)
    own_score = jnp.einsum("rkgd,rkd->rkg", query_head_rows, incoming_key) * scaling
    highest = jnp.maximum(jnp.max(scores, axis=-1), own_score)
    weights_cache = jnp.where(live_slot[:, None, None, :], jnp.exp(scores - highest[..., None]), 0.0)
    own_weight = jnp.exp(own_score - highest)
    totals = jnp.sum(weights_cache, axis=-1) + own_weight
    probs_cache = lax.optimization_barrier((weights_cache / totals[..., None]).astype(jnp.bfloat16)).astype(jnp.float32)
    probs_own = lax.optimization_barrier((own_weight / totals).astype(jnp.bfloat16)).astype(jnp.float32)
    mixed_values = jnp.einsum("rkgl,rlkd->rkgd", probs_cache, cache_value_rows)
    mixed_values = mixed_values + probs_own[..., None] * incoming_value[:, :, None, :]
    return mixed_values.reshape(request_batch, QUERY_HEADS * HEAD_SIZE).astype(jnp.bfloat16)


def reference(queries, incoming_pair, cache_key_value, cache_length, out_weight, adapter_down, adapter_up, request_adapter, adapter_slot):
    attended = attend(queries, incoming_pair, cache_key_value, cache_length)
    base_out = jnp.dot(attended, out_weight, preferred_element_type=jnp.float32)
    token_slot = adapter_slot[request_adapter].astype(jnp.int32)

    def shrink_one(packed):
        row_values, slot_index = packed
        factor = lax.dynamic_index_in_dim(adapter_down, slot_index, 0, keepdims=False)
        return jnp.dot(row_values[None, :], factor, preferred_element_type=jnp.float32)[0]

    def expand_one(packed):
        row_values, slot_index = packed
        factor = lax.dynamic_index_in_dim(adapter_up, slot_index, 0, keepdims=False)
        return jnp.dot(row_values[None, :], factor, preferred_element_type=jnp.float32)[0]

    shrunk = lax.map(shrink_one, (attended, token_slot)).astype(jnp.bfloat16)
    adapter_delta = lax.map(expand_one, (shrunk, token_slot))
    return (base_out + ADAPTER_GAIN * adapter_delta).astype(jnp.bfloat16)
```

```python
import functools

import jax
import jax.numpy as jnp
from jax import lax
from jax.experimental import pallas as pl
from jax.experimental.pallas import tpu as pltpu
from jax.sharding import PartitionSpec as P

QUERY_HEADS = 64
KEY_VALUE_HEADS = 8
HEAD_SIZE = 128
GROUP = QUERY_HEADS // KEY_VALUE_HEADS
WIDTH = QUERY_HEADS * HEAD_SIZE
LANES = 128
ADAPTER_GAIN = 2.0
MASKED_SCORE = -1e30

CUT = 5632

NT = (((1,), (1,)), ((), ()))
VMEM = pl.BlockSpec(memory_space=pltpu.VMEM)
SMEM = pl.BlockSpec(memory_space=pltpu.SMEM)


def attend_kernel(
    length_ref, adapter_ref, slot_ref, query_ref, pair_ref, cache_ref,
    a_ref, b_ref, cache, spread, mixed, sems,
):
    requests = query_ref.shape[0]
    slots = cache.shape[2]

    def fetch(r):
        return pltpu.make_async_copy(cache_ref.at[r], cache.at[r], sems.at[r])

    for r in range(requests):
        fetch(r).start()
    scaling = HEAD_SIZE ** (-0.5)
    for h in range(QUERY_HEADS):
        spread[pl.ds(h, requests, stride=QUERY_HEADS), :] = query_ref[
            :, h * HEAD_SIZE : (h + 1) * HEAD_SIZE
        ].astype(jnp.float32)
    position = lax.broadcasted_iota(jnp.int32, (QUERY_HEADS, slots), 1)
    blank = jnp.zeros((GROUP, HEAD_SIZE), jnp.float32)
    pairs = KEY_VALUE_HEADS // 2
    for r in range(requests):
        rows = spread[r * QUERY_HEADS : (r + 1) * QUERY_HEADS, :]
        new = pair_ref[r].astype(jnp.float32)
        own_key = jnp.concatenate(
            [
                jnp.broadcast_to(new[0:1, k * HEAD_SIZE : (k + 1) * HEAD_SIZE], (GROUP, HEAD_SIZE))
                for k in range(KEY_VALUE_HEADS)
            ],
            axis=0,
        )
        own_score = jnp.sum(rows * own_key, axis=1, keepdims=True) * scaling
        fetch(r).wait()
        scores = []
        for j in range(pairs):
            upper = rows[2 * j * GROUP : (2 * j + 1) * GROUP]
            lower = rows[(2 * j + 1) * GROUP : (2 * j + 2) * GROUP]
            both = jnp.concatenate(
                [
                    jnp.concatenate([upper, blank], axis=1),
                    jnp.concatenate([blank, lower], axis=1),
                ],
                axis=0,
            ).astype(jnp.bfloat16)
            keys = cache[r, 0, :, 2 * j * HEAD_SIZE : (2 * j + 2) * HEAD_SIZE]
            scores.append(lax.dot_general(both, keys, NT, preferred_element_type=jnp.float32))
        score = jnp.concatenate(scores, axis=0) * scaling
        live = position < length_ref[r]
        score = jnp.where(live, score, MASKED_SCORE)
        top = jnp.maximum(jnp.max(score, axis=1, keepdims=True), own_score)
        weight = jnp.where(live, jnp.exp(score - top), 0.0)
        own_weight = jnp.exp(own_score - top)
        total = jnp.sum(weight, axis=1, keepdims=True) + own_weight
        prob = (weight / total).astype(jnp.bfloat16)
        own_prob = (own_weight / total).astype(jnp.bfloat16).astype(jnp.float32)
        outs = []
        for j in range(pairs):
            values = cache[r, 1, :, 2 * j * HEAD_SIZE : (2 * j + 2) * HEAD_SIZE]
            both = jnp.dot(
                prob[2 * j * GROUP : (2 * j + 2) * GROUP], values,
                preferred_element_type=jnp.float32,
            )
            outs += [both[:GROUP, :HEAD_SIZE], both[GROUP:, HEAD_SIZE:]]
        own_value = jnp.concatenate(
            [
                jnp.broadcast_to(new[1:2, k * HEAD_SIZE : (k + 1) * HEAD_SIZE], (GROUP, HEAD_SIZE))
                for k in range(KEY_VALUE_HEADS)
            ],
            axis=0,
        )
        mixed[r * QUERY_HEADS : (r + 1) * QUERY_HEADS, :] = (
            jnp.concatenate(outs, axis=0) + own_prob * own_value
        )
    for h in range(QUERY_HEADS):
        column = h * HEAD_SIZE
        out = mixed[pl.ds(h, requests, stride=QUERY_HEADS), :].astype(jnp.bfloat16)
        if column < a_ref.shape[1]:
            a_ref[:, column : column + HEAD_SIZE] = out
        else:
            column -= a_ref.shape[1]
            b_ref[:, column : column + HEAD_SIZE] = out
    row = lax.broadcasted_iota(jnp.int32, (requests, LANES), 0)
    tag = jnp.zeros((requests, LANES), jnp.int32)
    for r in range(requests):
        tag = jnp.where(row == r, slot_ref[adapter_ref[r]], tag)
    b_ref[:, b_ref.shape[1] - LANES :] = tag.astype(jnp.float32).astype(jnp.bfloat16)


def attend(queries, incoming_pair, cache_key_value, cache_length, request_adapter, adapter_slot):
    requests = queries.shape[0]
    bf16 = jnp.bfloat16
    return pl.pallas_call(
        attend_kernel,
        out_shape=(
            jax.ShapeDtypeStruct((requests, CUT), bf16),
            jax.ShapeDtypeStruct((requests, WIDTH - CUT + LANES), bf16),
        ),
        in_specs=[SMEM, SMEM, SMEM, VMEM, VMEM, pl.BlockSpec(memory_space=pl.ANY)],
        out_specs=(VMEM, VMEM),
        scratch_shapes=[
            pltpu.VMEM(cache_key_value.shape, bf16),
            pltpu.VMEM((requests * QUERY_HEADS, HEAD_SIZE), jnp.float32),
            pltpu.VMEM((requests * QUERY_HEADS, HEAD_SIZE), jnp.float32),
            pltpu.SemaphoreType.DMA((requests,)),
        ],
        compiler_params=pltpu.CompilerParams(vmem_limit_bytes=24 << 20),
        name="attend",
    )(cache_length, request_adapter, adapter_slot, queries, incoming_pair, cache_key_value)


def shrink_kernel(device_ref, rows_ref, other_ref, down_ref, head_ref, shrunk_ref):
    held, rank = down_ref.shape[0], down_ref.shape[1]
    half = rows_ref.shape[0]
    head = head_ref.shape[1]
    device = device_ref[0]
    down = down_ref[...].reshape(held * rank, WIDTH)
    start = pl.multiple_of(device * head, head)
    for i, ref in enumerate((rows_ref, other_ref)):
        at = slice(i * half, (i + 1) * half)
        terms = lax.dot_general(ref[:, :WIDTH], down, NT, preferred_element_type=jnp.float32)
        column = lax.broadcasted_iota(jnp.int32, (half, held * rank), 1)
        slot = ref[:, WIDTH : WIDTH + LANES].astype(jnp.float32)[:, :1]
        own = (device * held + column // rank).astype(jnp.float32)
        shrunk = jnp.where(slot == own, terms, 0.0).astype(jnp.bfloat16)
        shrunk_ref[at, :] = shrunk * jnp.bfloat16(ADAPTER_GAIN)
        head_ref[at, :] = ref[:, pl.ds(start, head)]


def shrink(device, rows, other, down, head):
    half = rows.shape[0]
    held, rank = down.shape[0], down.shape[1]
    bf16 = jnp.bfloat16
    return pl.pallas_call(
        shrink_kernel,
        out_shape=(
            jax.ShapeDtypeStruct((2 * half, head), bf16),
            jax.ShapeDtypeStruct((2 * half, held * rank), bf16),
        ),
        in_specs=[SMEM, VMEM, VMEM, VMEM],
        out_specs=(VMEM, VMEM),
        compiler_params=pltpu.CompilerParams(vmem_limit_bytes=24 << 20),
        name="shrink",
    )(device, rows, other, down)


def project_kernel(head_ref, shrunk_ref, weight_ref, up_ref, own_ref, other_ref):
    half = own_ref.shape[0]
    held, rank, tile = up_ref.shape
    out = jnp.dot(head_ref[...], weight_ref[...], preferred_element_type=jnp.float32)
    out += jnp.dot(
        shrunk_ref[...], up_ref[...].reshape(held * rank, tile),
        preferred_element_type=jnp.float32,
    )
    own_ref[...] = out[:half]
    other_ref[...] = out[half:].astype(jnp.bfloat16)


def project(head, shrunk, weight, up, first, columns, tile):
    rows = head.shape[0]
    half = rows // 2
    skip = first // tile
    held, rank = up.shape[0], up.shape[1]
    return pl.pallas_call(
        project_kernel,
        grid=(columns // tile,),
        out_shape=(
            jax.ShapeDtypeStruct((half, columns), jnp.float32),
            jax.ShapeDtypeStruct((half, columns), jnp.bfloat16),
        ),
        in_specs=[
            pl.BlockSpec(head.shape, lambda i: (0, 0)),
            pl.BlockSpec(shrunk.shape, lambda i: (0, 0)),
            pl.BlockSpec((weight.shape[0], tile), lambda i: (0, i + skip)),
            pl.BlockSpec((held, rank, tile), lambda i: (0, 0, i + skip)),
        ],
        out_specs=(
            pl.BlockSpec((half, tile), lambda i: (0, i)),
            pl.BlockSpec((half, tile), lambda i: (0, i)),
        ),
        compiler_params=pltpu.CompilerParams(vmem_limit_bytes=32 << 20),
        name="project",
    )(head, shrunk, weight, up)


def per_device(
    queries, incoming_pair, cache_key_value, cache_length, out_weight,
    adapter_down, adapter_up, request_adapter, adapter_slot, *, members,
):
    depths = members // 4
    f32, bf16 = jnp.float32, jnp.bfloat16

    def swap(x, mask):
        return lax.ppermute(x, "rep", [(i, i ^ mask) for i in range(members)])

    requests = queries.shape[0]
    a, b = attend(
        queries, incoming_pair, cache_key_value, cache_length, request_adapter, adapter_slot
    )

    b_sides = jnp.concatenate([b, swap(b, 2)], axis=0)
    a_depths = jnp.concatenate([a] + [swap(a, 4 * d) for d in range(1, depths)], axis=0)
    a_all = jnp.concatenate([a_depths, swap(a_depths, 2)], axis=0)
    b_all = jnp.stack([b_sides] + [swap(b_sides, 4 * d) for d in range(1, depths)], axis=0)
    b_all = jnp.swapaxes(b_all.reshape(depths, 2, requests, -1), 0, 1)
    rows = jnp.concatenate([a_all, b_all.reshape(2 * depths * requests, -1)], axis=1)
    other = swap(rows, 1)

    device = lax.axis_index("rep").astype(jnp.int32).reshape(1)
    head, shrunk = shrink(
        device, rows, other, jnp.swapaxes(adapter_down, 1, 2), out_weight.shape[0]
    )

    b_width = WIDTH - CUT
    b_own, b_other = project(head, shrunk, out_weight, adapter_up, CUT, b_width, 512)
    b_sum = (b_own + swap(b_other, 1).astype(f32)).reshape(2, depths, requests, b_width)
    a_own, a_other = project(head, shrunk, out_weight, adapter_up, 0, CUT, 512)
    b_send = b_sum.astype(bf16)
    b_part = b_sum[:, 0]
    for d in range(1, depths):
        b_part = b_part + swap(b_send[:, d], 4 * d).astype(f32)
    a_sum = (a_own + swap(a_other, 1).astype(f32)).reshape(2, depths, requests, CUT)
    a_part = a_sum[0] + swap(a_sum[1].astype(bf16), 2).astype(f32)
    a_send = a_part.astype(bf16)
    a_out = a_part[0]
    for d in range(1, depths):
        a_out = a_out + swap(a_send[d], 4 * d).astype(f32)
    b_out = b_part[0] + swap(b_part[1].astype(bf16), 2).astype(f32)
    return jnp.concatenate([a_out, b_out], axis=1).astype(bf16)


def solution(mesh):
    in_specs = (
        P(("groups", "rep"), None),
        P(("groups", "rep"), None, None),
        P(("groups", "rep"), None, None, None),
        P(("groups", "rep")),
        P("rep", None),
        P(("groups", "rep"), None, None),
        P(("groups", "rep"), None, None),
        P(("groups", "rep")),
        P("groups"),
    )
    out_specs = P(("groups", "rep"), None)
    return jax.shard_map(
        functools.partial(per_device, members=mesh.shape["rep"]),
        mesh=mesh, in_specs=in_specs, out_specs=out_specs, check_vma=False,
    )
```

```python
import functools

import jax
import jax.numpy as jnp
from jax import lax
from jax.experimental import pallas as pl
from jax.experimental.pallas import tpu as pltpu
from jax.sharding import PartitionSpec as P

QUERY_HEADS = 64
KEY_VALUE_HEADS = 8
HEAD_SIZE = 128
GROUP = QUERY_HEADS // KEY_VALUE_HEADS
WIDTH = QUERY_HEADS * HEAD_SIZE
LANES = 128
ADAPTER_GAIN = 2.0
MASKED_SCORE = -1e30

CUT = 5632

NT = (((1,), (1,)), ((), ()))
VMEM = pl.BlockSpec(memory_space=pltpu.VMEM)
HBM = pl.BlockSpec(memory_space=pltpu.HBM)
SMEM = pl.BlockSpec(memory_space=pltpu.SMEM)


def held_in_vmem(x):
    return pltpu.with_memory_space_constraint(x, pltpu.VMEM)


def cost(flops, size):
    return pl.CostEstimate(flops=flops, bytes_accessed=size, transcendentals=0)


def attend_kernel(
    length_hbm, adapter_hbm, slot_hbm, query_hbm, pair_hbm, cache_hbm, a_ref, b_ref,
    length_ref, adapter_ref, slot_ref, query_ref, pair_ref, cache, spread, mixed, sems,
):
    requests = query_ref.shape[0]
    slots = cache.shape[2]

    def fetch(r):
        return pltpu.make_async_copy(cache_hbm.at[r], cache.at[r], sems.at[r])

    small = [
        pltpu.make_async_copy(source, target, sems.at[requests + i])
        for i, (source, target) in enumerate(
            (
                (query_hbm, query_ref), (pair_hbm, pair_ref), (length_hbm, length_ref),
                (adapter_hbm, adapter_ref), (slot_hbm, slot_ref),
            )
        )
    ]
    for copy in small:
        copy.start()
    for r in range(requests):
        fetch(r).start()
    for copy in small:
        copy.wait()
    scaling = HEAD_SIZE ** (-0.5)
    for h in range(QUERY_HEADS):
        spread[pl.ds(h, requests, stride=QUERY_HEADS), :] = query_ref[
            :, h * HEAD_SIZE : (h + 1) * HEAD_SIZE
        ].astype(jnp.float32)
    position = lax.broadcasted_iota(jnp.int32, (QUERY_HEADS, slots), 1)
    blank = jnp.zeros((GROUP, HEAD_SIZE), jnp.float32)
    pairs = KEY_VALUE_HEADS // 2
    for r in range(requests):
        rows = spread[r * QUERY_HEADS : (r + 1) * QUERY_HEADS, :]
        new = pair_ref[r].astype(jnp.float32)
        own_key = jnp.concatenate(
            [
                jnp.broadcast_to(new[0:1, k * HEAD_SIZE : (k + 1) * HEAD_SIZE], (GROUP, HEAD_SIZE))
                for k in range(KEY_VALUE_HEADS)
            ],
            axis=0,
        )
        own_score = jnp.sum(rows * own_key, axis=1, keepdims=True) * scaling
        fetch(r).wait()
        scores = []
        for j in range(pairs):
            upper = rows[2 * j * GROUP : (2 * j + 1) * GROUP]
            lower = rows[(2 * j + 1) * GROUP : (2 * j + 2) * GROUP]
            both = jnp.concatenate(
                [
                    jnp.concatenate([upper, blank], axis=1),
                    jnp.concatenate([blank, lower], axis=1),
                ],
                axis=0,
            ).astype(jnp.bfloat16)
            keys = cache[r, 0, :, 2 * j * HEAD_SIZE : (2 * j + 2) * HEAD_SIZE]
            scores.append(lax.dot_general(both, keys, NT, preferred_element_type=jnp.float32))
        score = jnp.concatenate(scores, axis=0) * scaling
        live = position < length_ref[r]
        score = jnp.where(live, score, MASKED_SCORE)
        top = jnp.maximum(jnp.max(score, axis=1, keepdims=True), own_score)
        weight = jnp.where(live, jnp.exp(score - top), 0.0)
        own_weight = jnp.exp(own_score - top)
        total = jnp.sum(weight, axis=1, keepdims=True) + own_weight
        prob = (weight / total).astype(jnp.bfloat16)
        own_prob = (own_weight / total).astype(jnp.bfloat16).astype(jnp.float32)
        outs = []
        for j in range(pairs):
            values = cache[r, 1, :, 2 * j * HEAD_SIZE : (2 * j + 2) * HEAD_SIZE]
            both = jnp.dot(
                prob[2 * j * GROUP : (2 * j + 2) * GROUP], values,
                preferred_element_type=jnp.float32,
            )
            outs += [both[:GROUP, :HEAD_SIZE], both[GROUP:, HEAD_SIZE:]]
        own_value = jnp.concatenate(
            [
                jnp.broadcast_to(new[1:2, k * HEAD_SIZE : (k + 1) * HEAD_SIZE], (GROUP, HEAD_SIZE))
                for k in range(KEY_VALUE_HEADS)
            ],
            axis=0,
        )
        mixed[r * QUERY_HEADS : (r + 1) * QUERY_HEADS, :] = (
            jnp.concatenate(outs, axis=0) + own_prob * own_value
        )
    for h in range(QUERY_HEADS):
        column = h * HEAD_SIZE
        out = mixed[pl.ds(h, requests, stride=QUERY_HEADS), :].astype(jnp.bfloat16)
        if column < a_ref.shape[1]:
            a_ref[:, column : column + HEAD_SIZE] = out
        else:
            column -= a_ref.shape[1]
            b_ref[:, column : column + HEAD_SIZE] = out
    row = lax.broadcasted_iota(jnp.int32, (requests, LANES), 0)
    tag = jnp.zeros((requests, LANES), jnp.int32)
    for r in range(requests):
        tag = jnp.where(row == r, slot_ref[adapter_ref[r]], tag)
    b_ref[:, b_ref.shape[1] - LANES :] = tag.astype(jnp.float32).astype(jnp.bfloat16)


def attend(queries, incoming_pair, cache_key_value, cache_length, request_adapter, adapter_slot):
    requests = queries.shape[0]
    bf16, f32 = jnp.bfloat16, jnp.float32
    ints = (cache_length, request_adapter, adapter_slot)
    inputs = ints + (queries, incoming_pair, cache_key_value)
    return pl.pallas_call(
        attend_kernel,
        out_shape=(
            pltpu.VMEM((requests, CUT), bf16),
            pltpu.VMEM((requests, WIDTH - CUT + LANES), bf16),
        ),
        in_specs=[HBM] * 6,
        out_specs=(VMEM,) * 2,
        scratch_shapes=[pltpu.SMEM(x.shape, jnp.int32) for x in ints]
        + [
            pltpu.VMEM(queries.shape, bf16),
            pltpu.VMEM(incoming_pair.shape, bf16),
            pltpu.VMEM(cache_key_value.shape, bf16),
            pltpu.VMEM((requests * QUERY_HEADS, HEAD_SIZE), f32),
            pltpu.VMEM((requests * QUERY_HEADS, HEAD_SIZE), f32),
            pltpu.SemaphoreType.DMA((requests + 5,)),
        ],
        compiler_params=pltpu.CompilerParams(vmem_limit_bytes=20 << 20),
        cost_estimate=cost(10**9, 2 * cache_key_value.size),
        name="attend",
    )(*(pltpu.with_memory_space_constraint(x, pltpu.HBM) for x in inputs))


def shrink_kernel(device_ref, rows_ref, down_ref, down_other_ref, own_ref, other_ref):
    held, rank = down_ref.shape[0], down_ref.shape[1]
    half = rows_ref.shape[0]
    ranks = held * rank
    head = own_ref.shape[1] - ranks
    me = device_ref[0]
    slot = rows_ref[:, WIDTH : WIDTH + LANES].astype(jnp.float32)[:, :1]
    column = lax.broadcasted_iota(jnp.int32, (half, ranks), 1)
    for device, factor, ref in ((me, down_ref, own_ref), (me ^ 1, down_other_ref, other_ref)):
        terms = lax.dot_general(
            rows_ref[:, :WIDTH], factor[...].reshape(ranks, WIDTH), NT,
            preferred_element_type=jnp.float32,
        )
        owned = (device * held + column // rank).astype(jnp.float32)
        shrunk = jnp.where(slot == owned, terms, 0.0).astype(jnp.bfloat16)
        ref[:, head:] = shrunk * jnp.bfloat16(ADAPTER_GAIN)
        ref[:, :head] = rows_ref[:, pl.ds(pl.multiple_of(device * head, head), head)]


def shrink(device, rows, down, down_other, head):
    half = rows.shape[0]
    ranks = down.shape[0] * down.shape[1]
    out = jax.ShapeDtypeStruct((half, head + ranks), jnp.bfloat16)
    return pl.pallas_call(
        shrink_kernel,
        out_shape=(out, out),
        in_specs=[SMEM, VMEM, VMEM, VMEM],
        out_specs=(VMEM, VMEM),
        compiler_params=pltpu.CompilerParams(vmem_limit_bytes=16 << 20),
        cost_estimate=cost(4 * half * ranks * WIDTH, 4 * ranks * WIDTH),
        name="shrink",
    )(device, rows, held_in_vmem(down), down_other)


def project_kernel(tile, x_ref, x_other_ref, weight_ref, up_ref, own_ref, other_ref):
    half, columns = own_ref.shape
    held, rank, _ = up_ref.shape
    head = weight_ref.shape[0]
    x = jnp.concatenate([x_other_ref[...], x_ref[...]], axis=0)
    for start in range(0, columns, tile):
        at = slice(start, start + tile)
        out = jnp.dot(x[:, :head], weight_ref[:, at], preferred_element_type=jnp.float32)
        out += jnp.dot(
            x[:, head:], up_ref[:, :, at].reshape(held * rank, tile),
            preferred_element_type=jnp.float32,
        )
        other_ref[:, at] = out[:half].astype(jnp.bfloat16)
        own_ref[:, at] = out[half:]


def project(x, x_other, weight, up):
    half, columns = x.shape[0], weight.shape[1]
    return pl.pallas_call(
        functools.partial(project_kernel, 512),
        out_shape=(
            jax.ShapeDtypeStruct((half, columns), jnp.float32),
            jax.ShapeDtypeStruct((half, columns), jnp.bfloat16),
        ),
        in_specs=[VMEM] * 4,
        out_specs=(VMEM, VMEM),
        compiler_params=pltpu.CompilerParams(vmem_limit_bytes=16 << 20),
        cost_estimate=cost(4 * half * x.shape[1] * columns, 2 * x.shape[1] * columns),
        name="project",
    )(x, x_other, held_in_vmem(weight), held_in_vmem(up))


def per_device(
    queries, incoming_pair, cache_key_value, cache_length, out_weight,
    adapter_down, adapter_up, request_adapter, adapter_slot, *, members,
):
    depths = members // 4
    f32, bf16 = jnp.float32, jnp.bfloat16

    def swap(x, mask):
        return lax.ppermute(x, "rep", [(i, i ^ mask) for i in range(members)])

    requests = queries.shape[0]
    down = jnp.swapaxes(adapter_down, 1, 2)
    down_other = swap(down, 1)
    a, b = attend(
        queries, incoming_pair, cache_key_value, cache_length, request_adapter, adapter_slot
    )

    b_sides = jnp.concatenate([b, swap(b, 2)], axis=0)
    a_depths = jnp.concatenate([a] + [swap(a, 4 * d) for d in range(1, depths)], axis=0)
    a_all = jnp.concatenate([a_depths, swap(a_depths, 2)], axis=0)
    b_all = jnp.stack([b_sides] + [swap(b_sides, 4 * d) for d in range(1, depths)], axis=0)
    b_all = jnp.swapaxes(b_all.reshape(depths, 2, requests, -1), 0, 1)
    rows = jnp.concatenate([a_all, b_all.reshape(2 * depths * requests, -1)], axis=1)

    device = lax.axis_index("rep").astype(jnp.int32).reshape(1)
    x, x_send = shrink(device, rows, down, down_other, out_weight.shape[0])
    x_other = swap(x_send, 1)

    own, send = project(x, x_other, out_weight, adapter_up)
    sums = (own + swap(send, 1).astype(f32)).reshape(2, depths, requests, WIDTH)
    a_sum, b_sum = sums[..., :CUT], sums[..., CUT:]
    a_part = a_sum[0] + swap(a_sum[1].astype(bf16), 2).astype(f32)
    b_send = b_sum.astype(bf16)
    b_part = b_sum[:, 0]
    for d in range(1, depths):
        b_part = b_part + swap(b_send[:, d], 4 * d).astype(f32)
    a_send = a_part.astype(bf16)
    a_out = a_part[0]
    for d in range(1, depths):
        a_out = a_out + swap(a_send[d], 4 * d).astype(f32)
    b_out = b_part[0] + swap(b_part[1].astype(bf16), 2).astype(f32)
    return jnp.concatenate([a_out, b_out], axis=1).astype(bf16)


def solution(mesh):
    in_specs = (
        P(("groups", "rep"), None),
        P(("groups", "rep"), None, None),
        P(("groups", "rep"), None, None, None),
        P(("groups", "rep")),
        P("rep", None),
        P(("groups", "rep"), None, None),
        P(("groups", "rep"), None, None),
        P(("groups", "rep")),
        P("groups"),
    )
    out_specs = P(("groups", "rep"), None)
    return jax.shard_map(
        functools.partial(per_device, members=mesh.shape["rep"]),
        mesh=mesh, in_specs=in_specs, out_specs=out_specs, check_vma=False,
    )
```

```python
import functools

import jax
import jax.numpy as jnp
from jax import lax
from jax.experimental import pallas as pl
from jax.experimental.pallas import tpu as pltpu
from jax.sharding import PartitionSpec as P

QUERY_HEADS = 64
KEY_VALUE_HEADS = 8
HEAD_SIZE = 128
GROUP = QUERY_HEADS // KEY_VALUE_HEADS
WIDTH = QUERY_HEADS * HEAD_SIZE
LANES = 128
BATCH = 4
ADAPTER_GAIN = 2.0
MASKED_SCORE = -1e30

CUT = 5888

NT = (((1,), (1,)), ((), ()))
VMEM = pl.BlockSpec(memory_space=pltpu.VMEM)
HBM = pl.BlockSpec(memory_space=pltpu.HBM)
SMEM = pl.BlockSpec(memory_space=pltpu.SMEM)


def held_in_vmem(x):
    return pltpu.with_memory_space_constraint(x, pltpu.VMEM)


def cost(flops, size):
    return pl.CostEstimate(flops=flops, bytes_accessed=size, transcendentals=0)


def per_head(row):
    return jnp.concatenate(
        [
            jnp.broadcast_to(row[:, k * HEAD_SIZE : (k + 1) * HEAD_SIZE], (GROUP, HEAD_SIZE))
            for k in range(KEY_VALUE_HEADS)
        ],
        axis=0,
    )


def attend_kernel(
    length_hbm, adapter_hbm, slot_hbm, query_hbm, pair_hbm, cache_hbm, a_ref, all_ref,
    length_ref, adapter_ref, slot_ref, query_ref, pair_ref, cache, spread, mixed, sems,
):
    requests = query_ref.shape[0]
    slots = cache.shape[2]

    def fetch(r):
        return pltpu.make_async_copy(cache_hbm.at[r], cache.at[r], sems.at[r])

    small = [
        pltpu.make_async_copy(source, target, sems.at[requests + i])
        for i, (source, target) in enumerate(
            (
                (query_hbm, query_ref), (pair_hbm, pair_ref), (length_hbm, length_ref),
                (adapter_hbm, adapter_ref), (slot_hbm, slot_ref),
            )
        )
    ]
    for copy in small:
        copy.start()
    for r in range(requests):
        fetch(r).start()
    for copy in small:
        copy.wait()
    scaling = HEAD_SIZE ** (-0.5)
    for h in range(QUERY_HEADS):
        spread[pl.ds(h, requests, stride=QUERY_HEADS), :] = query_ref[
            :, h * HEAD_SIZE : (h + 1) * HEAD_SIZE
        ].astype(jnp.float32)
    position = lax.broadcasted_iota(jnp.int32, (QUERY_HEADS, slots), 1)
    blank = jnp.zeros((GROUP, HEAD_SIZE), jnp.float32)
    pairs = KEY_VALUE_HEADS // 2
    for r in range(0, requests, BATCH):
        batch = range(r, r + BATCH)
        for t in batch:
            fetch(t).wait()
        scores = []
        for t in batch:
            rows = spread[t * QUERY_HEADS : (t + 1) * QUERY_HEADS, :]
            parts = []
            for j in range(pairs):
                upper = rows[2 * j * GROUP : (2 * j + 1) * GROUP]
                lower = rows[(2 * j + 1) * GROUP : (2 * j + 2) * GROUP]
                both = jnp.concatenate(
                    [
                        jnp.concatenate([upper, blank], axis=1),
                        jnp.concatenate([blank, lower], axis=1),
                    ],
                    axis=0,
                ).astype(jnp.bfloat16)
                keys = cache[t, 0, :, 2 * j * HEAD_SIZE : (2 * j + 2) * HEAD_SIZE]
                parts.append(lax.dot_general(both, keys, NT, preferred_element_type=jnp.float32))
            live = position < length_ref[t]
            score = jnp.concatenate(parts, axis=0) * scaling
            scores.append((rows, live, jnp.where(live, score, MASKED_SCORE)))
        probs = []
        for t, (rows, live, score) in zip(batch, scores):
            new = pair_ref[t].astype(jnp.float32)
            own_score = jnp.sum(rows * per_head(new[0:1]), axis=1, keepdims=True) * scaling
            top = jnp.maximum(jnp.max(score, axis=1, keepdims=True), own_score)
            weight = jnp.where(live, jnp.exp(score - top), 0.0)
            own_weight = jnp.exp(own_score - top)
            total = jnp.sum(weight, axis=1, keepdims=True) + own_weight
            prob = (weight / total).astype(jnp.bfloat16)
            own_prob = (own_weight / total).astype(jnp.bfloat16).astype(jnp.float32)
            probs.append((prob, own_prob * per_head(new[1:2])))
        for t, (prob, own_part) in zip(batch, probs):
            outs = []
            for j in range(pairs):
                values = cache[t, 1, :, 2 * j * HEAD_SIZE : (2 * j + 2) * HEAD_SIZE]
                both = jnp.dot(
                    prob[2 * j * GROUP : (2 * j + 2) * GROUP], values,
                    preferred_element_type=jnp.float32,
                )
                outs += [both[:GROUP, :HEAD_SIZE], both[GROUP:, HEAD_SIZE:]]
            mixed[t * QUERY_HEADS : (t + 1) * QUERY_HEADS, :] = (
                jnp.concatenate(outs, axis=0) + own_part
            )
    for h in range(QUERY_HEADS):
        column = h * HEAD_SIZE
        out = mixed[pl.ds(h, requests, stride=QUERY_HEADS), :].astype(jnp.bfloat16)
        all_ref[:, column : column + HEAD_SIZE] = out
        if column < a_ref.shape[1]:
            a_ref[:, column : column + HEAD_SIZE] = out
    row = lax.broadcasted_iota(jnp.int32, (requests, LANES), 0)
    tag = jnp.zeros((requests, LANES), jnp.int32)
    for r in range(requests):
        tag = jnp.where(row == r, slot_ref[adapter_ref[r]], tag)
    all_ref[:, WIDTH:] = tag.astype(jnp.float32).astype(jnp.bfloat16)


def attend(queries, incoming_pair, cache_key_value, cache_length, request_adapter, adapter_slot):
    requests = queries.shape[0]
    bf16, f32 = jnp.bfloat16, jnp.float32
    ints = (cache_length, request_adapter, adapter_slot)
    inputs = ints + (queries, incoming_pair, cache_key_value)
    return pl.pallas_call(
        attend_kernel,
        out_shape=(
            pltpu.VMEM((requests, CUT), bf16),
            pltpu.VMEM((requests, WIDTH + LANES), bf16),
        ),
        in_specs=[HBM] * 6,
        out_specs=(VMEM,) * 2,
        scratch_shapes=[pltpu.SMEM(x.shape, jnp.int32) for x in ints]
        + [
            pltpu.VMEM(queries.shape, bf16),
            pltpu.VMEM(incoming_pair.shape, bf16),
            pltpu.VMEM(cache_key_value.shape, bf16),
            pltpu.VMEM((requests * QUERY_HEADS, HEAD_SIZE), f32),
            pltpu.VMEM((requests * QUERY_HEADS, HEAD_SIZE), f32),
            pltpu.SemaphoreType.DMA((requests + 5,)),
        ],
        compiler_params=pltpu.CompilerParams(vmem_limit_bytes=20 << 20),
        cost_estimate=cost(10**9, 2 * cache_key_value.size),
        name="attend",
    )(*(pltpu.with_memory_space_constraint(x, pltpu.HBM) for x in inputs))


def shrink_kernel(device_ref, rows_ref, down_ref, down_other_ref, up_ref, own_ref, other_ref):
    del up_ref
    held, rank = down_ref.shape[0], down_ref.shape[1]
    half = rows_ref.shape[0]
    ranks = held * rank
    head = own_ref.shape[1] - ranks
    me = device_ref[0]
    terms = jnp.zeros((half, 2 * ranks), jnp.float32)
    for k in range(0, WIDTH, 512):
        at = slice(k, k + 512)
        factors = jnp.concatenate(
            [ref[:, :, at].reshape(ranks, 512) for ref in (down_ref, down_other_ref)], axis=0
        )
        terms += lax.dot_general(
            rows_ref[:, at], factors, NT, preferred_element_type=jnp.float32
        )
    slot = rows_ref[:, WIDTH : WIDTH + LANES].astype(jnp.float32)[:, :1]
    column = lax.broadcasted_iota(jnp.int32, (half, ranks), 1)
    for i, (device, ref) in enumerate(((me, own_ref), (me ^ 1, other_ref))):
        owned = (device * held + column // rank).astype(jnp.float32)
        part = terms[:, i * ranks : (i + 1) * ranks]
        shrunk = jnp.where(slot == owned, part, 0.0).astype(jnp.bfloat16)
        ref[:, head:] = shrunk * jnp.bfloat16(ADAPTER_GAIN)
        ref[:, :head] = rows_ref[:, pl.ds(pl.multiple_of(device * head, head), head)]


def shrink(device, rows, down, down_other, up, head):
    half = rows.shape[0]
    ranks = down.shape[0] * down.shape[1]
    out = jax.ShapeDtypeStruct((half, head + ranks), jnp.bfloat16)
    return pl.pallas_call(
        shrink_kernel,
        out_shape=(out, out),
        in_specs=[SMEM] + [VMEM] * 4,
        out_specs=(VMEM, VMEM),
        compiler_params=pltpu.CompilerParams(vmem_limit_bytes=16 << 20),
        cost_estimate=cost(4 * half * ranks * WIDTH, 4 * ranks * WIDTH),
        name="shrink",
    )(device, rows, held_in_vmem(down), held_in_vmem(down_other), held_in_vmem(up))


def project_kernel(tile, x_ref, x_other_ref, weight_ref, up_ref, own_ref, other_ref):
    half, columns = own_ref.shape
    held, rank, _ = up_ref.shape
    head = weight_ref.shape[0]
    x = jnp.concatenate([x_other_ref[...], x_ref[...]], axis=0)
    for start in range(0, columns, tile):
        at = slice(start, start + tile)
        out = jnp.dot(x[:, :head], weight_ref[:, at], preferred_element_type=jnp.float32)
        out += jnp.dot(
            x[:, head:], up_ref[:, :, at].reshape(held * rank, tile),
            preferred_element_type=jnp.float32,
        )
        other_ref[:, at] = out[:half].astype(jnp.bfloat16)
        own_ref[:, at] = out[half:]


def project(x, x_other, weight, up):
    half, columns = x.shape[0], weight.shape[1]
    return pl.pallas_call(
        functools.partial(project_kernel, 512),
        out_shape=(
            jax.ShapeDtypeStruct((half, columns), jnp.float32),
            jax.ShapeDtypeStruct((half, columns), jnp.bfloat16),
        ),
        in_specs=[VMEM] * 4,
        out_specs=(VMEM, VMEM),
        compiler_params=pltpu.CompilerParams(vmem_limit_bytes=16 << 20),
        cost_estimate=cost(4 * half * x.shape[1] * columns, 2 * x.shape[1] * columns),
        name="project",
    )(x, x_other, held_in_vmem(weight), held_in_vmem(up))


def per_device(
    queries, incoming_pair, cache_key_value, cache_length, out_weight,
    adapter_down, adapter_up, request_adapter, adapter_slot, *, members,
):
    depths = members // 4
    f32, bf16 = jnp.float32, jnp.bfloat16

    def swap(x, mask):
        return lax.ppermute(x, "rep", [(i, i ^ mask) for i in range(members)])

    requests = queries.shape[0]
    down = jnp.swapaxes(adapter_down, 1, 2)
    down_other = swap(down, 1)
    a, own = attend(
        queries, incoming_pair, cache_key_value, cache_length, request_adapter, adapter_slot
    )

    apart = range(1, depths)
    a_far = jnp.concatenate([swap(a, 4 * d) for d in apart], axis=0)
    side = swap(own, 2)
    b_sides = jnp.concatenate([own[:, CUT:], side[:, CUT:]], axis=0)
    b_far = jnp.stack([swap(b_sides, 4 * d) for d in apart], axis=0)
    b_far = jnp.swapaxes(b_far.reshape(depths - 1, 2, requests, -1), 0, 1)
    b_far = b_far.reshape(2, (depths - 1) * requests, -1)
    rows = jnp.concatenate(
        [
            own, jnp.concatenate([a_far, b_far[0]], axis=1),
            side, jnp.concatenate([swap(a_far, 2), b_far[1]], axis=1),
        ],
        axis=0,
    )

    device = lax.axis_index("rep").astype(jnp.int32).reshape(1)
    x, x_send = shrink(device, rows, down, down_other, adapter_up, out_weight.shape[0])
    x_other = swap(x_send, 1)

    mine, send = project(x, x_other, out_weight, adapter_up)
    sums = (mine + swap(send, 1).astype(f32)).reshape(2, depths, requests, WIDTH)
    a_sum, b_sum = sums[..., :CUT], sums[..., CUT:]
    a_part = a_sum[0, 1:] + swap(a_sum[1, 1:].astype(bf16), 2).astype(f32)
    b_send = b_sum.astype(bf16)
    b_part = b_sum[:, 0]
    for d in apart:
        b_part = b_part + swap(b_send[:, d], 4 * d).astype(f32)
    a_send = a_part.astype(bf16)
    a_out = a_sum[0, 0]
    for d in apart:
        a_out = a_out + swap(a_send[d - 1], 4 * d).astype(f32)
    side = swap(jnp.concatenate([a_sum[1, 0], b_part[1]], axis=1).astype(bf16), 2)
    return (jnp.concatenate([a_out, b_part[0]], axis=1) + side.astype(f32)).astype(bf16)


def solution(mesh):
    in_specs = (
        P(("groups", "rep"), None),
        P(("groups", "rep"), None, None),
        P(("groups", "rep"), None, None, None),
        P(("groups", "rep")),
        P("rep", None),
        P(("groups", "rep"), None, None),
        P(("groups", "rep"), None, None),
        P(("groups", "rep")),
        P("groups"),
    )
    out_specs = P(("groups", "rep"), None)
    return jax.shard_map(
        functools.partial(per_device, members=mesh.shape["rep"]),
        mesh=mesh, in_specs=in_specs, out_specs=out_specs, check_vma=False,
    )
```

```python
import functools

import jax
import jax.numpy as jnp
from jax import lax
from jax.experimental import pallas as pl
from jax.experimental.pallas import tpu as pltpu
from jax.sharding import PartitionSpec as P

QUERY_HEADS = 64
KEY_VALUE_HEADS = 8
HEAD_SIZE = 128
GROUP = QUERY_HEADS // KEY_VALUE_HEADS
WIDTH = QUERY_HEADS * HEAD_SIZE
LANES = 128
BATCH = 4
ADAPTER_GAIN = 2.0
MASKED_SCORE = -1e30

CUT = 5888

NT = (((1,), (1,)), ((), ()))
VMEM = pl.BlockSpec(memory_space=pltpu.VMEM)
HBM = pl.BlockSpec(memory_space=pltpu.HBM)
SMEM = pl.BlockSpec(memory_space=pltpu.SMEM)


def held_in_vmem(x):
    return pltpu.with_memory_space_constraint(x, pltpu.VMEM)


def cost(flops, size):
    return pl.CostEstimate(flops=flops, bytes_accessed=size, transcendentals=0)


def per_head(row):
    return jnp.concatenate(
        [
            jnp.broadcast_to(row[:, k * HEAD_SIZE : (k + 1) * HEAD_SIZE], (GROUP, HEAD_SIZE))
            for k in range(KEY_VALUE_HEADS)
        ],
        axis=0,
    )


def attend_kernel(
    length_hbm, adapter_hbm, slot_hbm, query_hbm, pair_hbm, cache_hbm, a_ref, all_ref,
    length_ref, adapter_ref, slot_ref, query_ref, pair_ref, cache, spread, mixed, sems,
):
    requests = query_ref.shape[0]
    slots = cache.shape[2]

    def fetch(r):
        return pltpu.make_async_copy(cache_hbm.at[r], cache.at[r], sems.at[r])

    small = [
        pltpu.make_async_copy(source, target, sems.at[requests + i])
        for i, (source, target) in enumerate(
            (
                (query_hbm, query_ref), (pair_hbm, pair_ref), (length_hbm, length_ref),
                (adapter_hbm, adapter_ref), (slot_hbm, slot_ref),
            )
        )
    ]
    for copy in small:
        copy.start()
    for r in range(requests):
        fetch(r).start()
    for copy in small:
        copy.wait()
    scaling = HEAD_SIZE ** (-0.5)
    for h in range(QUERY_HEADS):
        spread[pl.ds(h, requests, stride=QUERY_HEADS), :] = query_ref[
            :, h * HEAD_SIZE : (h + 1) * HEAD_SIZE
        ].astype(jnp.float32)
    position = lax.broadcasted_iota(jnp.int32, (QUERY_HEADS, slots), 1)
    blank = jnp.zeros((GROUP, HEAD_SIZE), jnp.float32)
    pairs = KEY_VALUE_HEADS // 2
    for r in range(0, requests, BATCH):
        batch = range(r, r + BATCH)
        for t in batch:
            fetch(t).wait()
        scores = []
        for t in batch:
            rows = spread[t * QUERY_HEADS : (t + 1) * QUERY_HEADS, :]
            parts = []
            for j in range(pairs):
                upper = rows[2 * j * GROUP : (2 * j + 1) * GROUP]
                lower = rows[(2 * j + 1) * GROUP : (2 * j + 2) * GROUP]
                both = jnp.concatenate(
                    [
                        jnp.concatenate([upper, blank], axis=1),
                        jnp.concatenate([blank, lower], axis=1),
                    ],
                    axis=0,
                ).astype(jnp.bfloat16)
                keys = cache[t, 0, :, 2 * j * HEAD_SIZE : (2 * j + 2) * HEAD_SIZE]
                parts.append(lax.dot_general(both, keys, NT, preferred_element_type=jnp.float32))
            live = position < length_ref[t]
            score = jnp.concatenate(parts, axis=0) * scaling
            scores.append((rows, live, jnp.where(live, score, MASKED_SCORE)))
        probs = []
        for t, (rows, live, score) in zip(batch, scores):
            new = pair_ref[t].astype(jnp.float32)
            own_score = jnp.sum(rows * per_head(new[0:1]), axis=1, keepdims=True) * scaling
            top = jnp.maximum(jnp.max(score, axis=1, keepdims=True), own_score)
            weight = jnp.where(live, jnp.exp(score - top), 0.0)
            own_weight = jnp.exp(own_score - top)
            total = jnp.sum(weight, axis=1, keepdims=True) + own_weight
            prob = (weight / total).astype(jnp.bfloat16)
            own_prob = (own_weight / total).astype(jnp.bfloat16).astype(jnp.float32)
            probs.append((prob, own_prob * per_head(new[1:2])))
        for t, (prob, own_part) in zip(batch, probs):
            outs = []
            for j in range(pairs):
                values = cache[t, 1, :, 2 * j * HEAD_SIZE : (2 * j + 2) * HEAD_SIZE]
                both = jnp.dot(
                    prob[2 * j * GROUP : (2 * j + 2) * GROUP], values,
                    preferred_element_type=jnp.float32,
                )
                outs += [both[:GROUP, :HEAD_SIZE], both[GROUP:, HEAD_SIZE:]]
            mixed[t * QUERY_HEADS : (t + 1) * QUERY_HEADS, :] = (
                jnp.concatenate(outs, axis=0) + own_part
            )
    for h in range(QUERY_HEADS):
        column = h * HEAD_SIZE
        out = mixed[pl.ds(h, requests, stride=QUERY_HEADS), :].astype(jnp.bfloat16)
        all_ref[:, column : column + HEAD_SIZE] = out
        if column < a_ref.shape[1]:
            a_ref[:, column : column + HEAD_SIZE] = out
    row = lax.broadcasted_iota(jnp.int32, (requests, LANES), 0)
    tag = jnp.zeros((requests, LANES), jnp.int32)
    for r in range(requests):
        tag = jnp.where(row == r, slot_ref[adapter_ref[r]], tag)
    all_ref[:, WIDTH:] = tag.astype(jnp.float32).astype(jnp.bfloat16)


def attend(queries, incoming_pair, cache_key_value, cache_length, request_adapter, adapter_slot):
    requests = queries.shape[0]
    bf16, f32 = jnp.bfloat16, jnp.float32
    ints = (cache_length, request_adapter, adapter_slot)
    inputs = ints + (queries, incoming_pair, cache_key_value)
    return pl.pallas_call(
        attend_kernel,
        out_shape=(
            pltpu.VMEM((requests, CUT), bf16),
            pltpu.VMEM((requests, WIDTH + LANES), bf16),
        ),
        in_specs=[HBM] * 6,
        out_specs=(VMEM,) * 2,
        scratch_shapes=[pltpu.SMEM(x.shape, jnp.int32) for x in ints]
        + [
            pltpu.VMEM(queries.shape, bf16),
            pltpu.VMEM(incoming_pair.shape, bf16),
            pltpu.VMEM(cache_key_value.shape, bf16),
            pltpu.VMEM((requests * QUERY_HEADS, HEAD_SIZE), f32),
            pltpu.VMEM((requests * QUERY_HEADS, HEAD_SIZE), f32),
            pltpu.SemaphoreType.DMA((requests + 5,)),
        ],
        compiler_params=pltpu.CompilerParams(vmem_limit_bytes=20 << 20),
        cost_estimate=cost(10**9, 2 * cache_key_value.size),
        name="attend",
    )(*(pltpu.with_memory_space_constraint(x, pltpu.HBM) for x in inputs))


def stage_kernel(down_ref, down_other_ref, out_ref, held, sems):
    ranks = held.shape[1]
    copies = [
        pltpu.make_async_copy(ref, held.at[i], sems.at[i])
        for i, ref in enumerate((down_ref, down_other_ref))
    ]
    for copy in copies:
        copy.start()
    for i, copy in enumerate(copies):
        copy.wait()
        for k in range(0, WIDTH, 1024):
            out_ref[k : k + 1024, i * ranks : (i + 1) * ranks] = held[i, :, k : k + 1024].T


def stage(down, down_other):
    ranks = down.shape[0] * down.shape[1]
    pair = [x.reshape(ranks, WIDTH) for x in (down, down_other)]
    return pl.pallas_call(
        stage_kernel,
        out_shape=pltpu.VMEM((WIDTH, 2 * ranks), jnp.bfloat16),
        in_specs=[HBM] * 2,
        out_specs=VMEM,
        scratch_shapes=[
            pltpu.VMEM((2, ranks, WIDTH), jnp.bfloat16),
            pltpu.SemaphoreType.DMA((2,)),
        ],
        compiler_params=pltpu.CompilerParams(vmem_limit_bytes=16 << 20),
        cost_estimate=cost(10**8, 8 * ranks * WIDTH),
        name="stage",
    )(*(pltpu.with_memory_space_constraint(x, pltpu.HBM) for x in pair))


def shrink_kernel(device_ref, rows_ref, factors_ref, up_ref, own_ref, other_ref):
    held, rank = up_ref.shape[0], up_ref.shape[1]
    half = rows_ref.shape[0]
    ranks = held * rank
    head = own_ref.shape[1] - ranks
    me = device_ref[0]
    terms = jnp.dot(rows_ref[:, :WIDTH], factors_ref[...], preferred_element_type=jnp.float32)
    slot = rows_ref[:, WIDTH : WIDTH + LANES].astype(jnp.float32)[:, :1]
    column = lax.broadcasted_iota(jnp.int32, (half, ranks), 1)
    for i, (device, ref) in enumerate(((me, own_ref), (me ^ 1, other_ref))):
        owned = (device * held + column // rank).astype(jnp.float32)
        part = terms[:, i * ranks : (i + 1) * ranks]
        shrunk = jnp.where(slot == owned, part, 0.0).astype(jnp.bfloat16)
        ref[:, head:] = shrunk * jnp.bfloat16(ADAPTER_GAIN)
        ref[:, :head] = rows_ref[:, pl.ds(pl.multiple_of(device * head, head), head)]


def shrink(device, rows, factors, up, head):
    half = rows.shape[0]
    ranks = up.shape[0] * up.shape[1]
    out = jax.ShapeDtypeStruct((half, head + ranks), jnp.bfloat16)
    return pl.pallas_call(
        shrink_kernel,
        out_shape=(out, out),
        in_specs=[SMEM] + [VMEM] * 3,
        out_specs=(VMEM, VMEM),
        compiler_params=pltpu.CompilerParams(vmem_limit_bytes=16 << 20),
        cost_estimate=cost(4 * half * ranks * WIDTH, 4 * ranks * WIDTH),
        name="shrink",
    )(device, rows, held_in_vmem(factors), held_in_vmem(up))


def project_kernel(tile, x_ref, x_other_ref, weight_ref, up_ref, own_ref, other_ref):
    half, columns = own_ref.shape
    held, rank, _ = up_ref.shape
    head = weight_ref.shape[0]
    x = jnp.concatenate([x_other_ref[...], x_ref[...]], axis=0)
    for start in range(0, columns, tile):
        at = slice(start, start + tile)
        out = jnp.dot(x[:, :head], weight_ref[:, at], preferred_element_type=jnp.float32)
        out += jnp.dot(
            x[:, head:], up_ref[:, :, at].reshape(held * rank, tile),
            preferred_element_type=jnp.float32,
        )
        other_ref[:, at] = out[:half].astype(jnp.bfloat16)
        own_ref[:, at] = out[half:]


def project(x, x_other, weight, up):
    half, columns = x.shape[0], weight.shape[1]
    return pl.pallas_call(
        functools.partial(project_kernel, 512),
        out_shape=(
            jax.ShapeDtypeStruct((half, columns), jnp.float32),
            jax.ShapeDtypeStruct((half, columns), jnp.bfloat16),
        ),
        in_specs=[VMEM] * 4,
        out_specs=(VMEM, VMEM),
        compiler_params=pltpu.CompilerParams(vmem_limit_bytes=16 << 20),
        cost_estimate=cost(4 * half * x.shape[1] * columns, 2 * x.shape[1] * columns),
        name="project",
    )(x, x_other, held_in_vmem(weight), held_in_vmem(up))


def per_device(
    queries, incoming_pair, cache_key_value, cache_length, out_weight,
    adapter_down, adapter_up, request_adapter, adapter_slot, *, members,
):
    depths = members // 4
    f32, bf16 = jnp.float32, jnp.bfloat16

    def swap(x, mask):
        return lax.ppermute(x, "rep", [(i, i ^ mask) for i in range(members)])

    requests = queries.shape[0]
    a, own = attend(
        queries, incoming_pair, cache_key_value, cache_length, request_adapter, adapter_slot
    )

    down = jnp.swapaxes(adapter_down, 1, 2)
    down_other, a, own = lax.optimization_barrier((swap(down, 1), a, own))
    factors = stage(down, down_other)

    apart = range(depths - 1, 0, -1)
    a_far = jnp.concatenate([swap(a, 4 * d) for d in apart], axis=0)
    side = swap(own, 2)
    b_sides = jnp.concatenate([own[:, CUT:], side[:, CUT:]], axis=0)
    b_far = jnp.stack([swap(b_sides, 4 * d) for d in apart], axis=0)
    b_far = jnp.swapaxes(b_far.reshape(depths - 1, 2, requests, -1), 0, 1)
    b_far = b_far.reshape(2, (depths - 1) * requests, -1)
    a_side = swap(a_far, 2)
    rows = jnp.concatenate(
        [
            own, jnp.concatenate([a_far, b_far[0]], axis=1),
            side, jnp.concatenate([a_side, b_far[1]], axis=1),
        ],
        axis=0,
    )

    device = lax.axis_index("rep").astype(jnp.int32).reshape(1)
    x, x_send = shrink(device, rows, factors, adapter_up, out_weight.shape[0])
    x_other = swap(x_send, 1)

    mine, send = project(x, x_other, out_weight, adapter_up)
    sums = (mine + swap(send, 1).astype(f32)).reshape(2, depths, requests, WIDTH)
    a_sum, b_sum = sums[..., :CUT], sums[..., CUT:]
    a_part = a_sum[0, 1:] + swap(a_sum[1, 1:].astype(bf16), 2).astype(f32)
    b_send = b_sum.astype(bf16)
    a_send = a_part.astype(bf16)
    b_came = [swap(b_send[:, i], 4 * d) for i, d in enumerate(apart, 1)]
    b_came, _ = lax.optimization_barrier((b_came, a_send))
    b_part = b_sum[:, 0]
    for came in b_came:
        b_part = b_part + came.astype(f32)
    a_out = a_sum[0, 0]
    for i, d in enumerate(apart):
        a_out = a_out + swap(a_send[i], 4 * d).astype(f32)
    side = swap(jnp.concatenate([a_sum[1, 0], b_part[1]], axis=1).astype(bf16), 2)
    return (jnp.concatenate([a_out, b_part[0]], axis=1) + side.astype(f32)).astype(bf16)


def solution(mesh):
    in_specs = (
        P(("groups", "rep"), None),
        P(("groups", "rep"), None, None),
        P(("groups", "rep"), None, None, None),
        P(("groups", "rep")),
        P("rep", None),
        P(("groups", "rep"), None, None),
        P(("groups", "rep"), None, None),
        P(("groups", "rep")),
        P("groups"),
    )
    out_specs = P(("groups", "rep"), None)
    return jax.shard_map(
        functools.partial(per_device, members=mesh.shape["rep"]),
        mesh=mesh, in_specs=in_specs, out_specs=out_specs, check_vma=False,
    )
```

```python
import functools

import jax
import jax.numpy as jnp
from jax import lax
from jax.experimental import pallas as pl
from jax.experimental.pallas import tpu as pltpu
from jax.sharding import PartitionSpec as P

QUERY_HEADS = 64
KEY_VALUE_HEADS = 8
HEAD_SIZE = 128
GROUP = QUERY_HEADS // KEY_VALUE_HEADS
WIDTH = QUERY_HEADS * HEAD_SIZE
LANES = 128
BATCH = 4
ADAPTER_GAIN = 2.0
MASKED_SCORE = -1e30

GATHER_CUT = 6144
SCATTER_CUT = 6144

NT = (((1,), (1,)), ((), ()))
VMEM = pl.BlockSpec(memory_space=pltpu.VMEM)
HBM = pl.BlockSpec(memory_space=pltpu.HBM)
SMEM = pl.BlockSpec(memory_space=pltpu.SMEM)


def held_in_vmem(x):
    return pltpu.with_memory_space_constraint(x, pltpu.VMEM)


def cost(flops, size):
    return pl.CostEstimate(flops=flops, bytes_accessed=size, transcendentals=0)


def per_head(row):
    return jnp.concatenate(
        [
            jnp.broadcast_to(row[:, k * HEAD_SIZE : (k + 1) * HEAD_SIZE], (GROUP, HEAD_SIZE))
            for k in range(KEY_VALUE_HEADS)
        ],
        axis=0,
    )


def attend_kernel(
    length_hbm, adapter_hbm, slot_hbm, query_hbm, pair_hbm, cache_hbm, a_ref, all_ref,
    length_ref, adapter_ref, slot_ref, query_ref, pair_ref, cache, spread, mixed, sems,
):
    requests = query_ref.shape[0]
    slots = cache.shape[2]

    def fetch(r):
        return pltpu.make_async_copy(cache_hbm.at[r], cache.at[r], sems.at[r])

    small = [
        pltpu.make_async_copy(source, target, sems.at[requests + i])
        for i, (source, target) in enumerate(
            (
                (query_hbm, query_ref), (pair_hbm, pair_ref), (length_hbm, length_ref),
                (adapter_hbm, adapter_ref), (slot_hbm, slot_ref),
            )
        )
    ]
    for copy in small:
        copy.start()
    for r in range(requests):
        fetch(r).start()
    for copy in small:
        copy.wait()
    scaling = HEAD_SIZE ** (-0.5)
    for h in range(QUERY_HEADS):
        spread[pl.ds(h, requests, stride=QUERY_HEADS), :] = query_ref[
            :, h * HEAD_SIZE : (h + 1) * HEAD_SIZE
        ].astype(jnp.float32)
    position = lax.broadcasted_iota(jnp.int32, (QUERY_HEADS, slots), 1)
    blank = jnp.zeros((GROUP, HEAD_SIZE), jnp.float32)
    pairs = KEY_VALUE_HEADS // 2
    for r in range(0, requests, BATCH):
        batch = range(r, r + BATCH)
        for t in batch:
            fetch(t).wait()
        scores = []
        for t in batch:
            rows = spread[t * QUERY_HEADS : (t + 1) * QUERY_HEADS, :]
            parts = []
            for j in range(pairs):
                upper = rows[2 * j * GROUP : (2 * j + 1) * GROUP]
                lower = rows[(2 * j + 1) * GROUP : (2 * j + 2) * GROUP]
                both = jnp.concatenate(
                    [
                        jnp.concatenate([upper, blank], axis=1),
                        jnp.concatenate([blank, lower], axis=1),
                    ],
                    axis=0,
                ).astype(jnp.bfloat16)
                keys = cache[t, 0, :, 2 * j * HEAD_SIZE : (2 * j + 2) * HEAD_SIZE]
                parts.append(lax.dot_general(both, keys, NT, preferred_element_type=jnp.float32))
            live = position < length_ref[t]
            score = jnp.concatenate(parts, axis=0) * scaling
            scores.append((rows, live, jnp.where(live, score, MASKED_SCORE)))
        probs = []
        for t, (rows, live, score) in zip(batch, scores):
            new = pair_ref[t].astype(jnp.float32)
            own_score = jnp.sum(rows * per_head(new[0:1]), axis=1, keepdims=True) * scaling
            top = jnp.maximum(jnp.max(score, axis=1, keepdims=True), own_score)
            weight = jnp.where(live, jnp.exp(score - top), 0.0)
            own_weight = jnp.exp(own_score - top)
            total = jnp.sum(weight, axis=1, keepdims=True) + own_weight
            prob = (weight / total).astype(jnp.bfloat16)
            own_prob = (own_weight / total).astype(jnp.bfloat16).astype(jnp.float32)
            probs.append((prob, own_prob * per_head(new[1:2])))
        for t, (prob, own_part) in zip(batch, probs):
            outs = []
            for j in range(pairs):
                values = cache[t, 1, :, 2 * j * HEAD_SIZE : (2 * j + 2) * HEAD_SIZE]
                both = jnp.dot(
                    prob[2 * j * GROUP : (2 * j + 2) * GROUP], values,
                    preferred_element_type=jnp.float32,
                )
                outs += [both[:GROUP, :HEAD_SIZE], both[GROUP:, HEAD_SIZE:]]
            mixed[t * QUERY_HEADS : (t + 1) * QUERY_HEADS, :] = (
                jnp.concatenate(outs, axis=0) + own_part
            )
    for h in range(QUERY_HEADS):
        column = h * HEAD_SIZE
        out = mixed[pl.ds(h, requests, stride=QUERY_HEADS), :].astype(jnp.bfloat16)
        all_ref[:, column : column + HEAD_SIZE] = out
        if column < a_ref.shape[1]:
            a_ref[:, column : column + HEAD_SIZE] = out
    row = lax.broadcasted_iota(jnp.int32, (requests, LANES), 0)
    tag = jnp.zeros((requests, LANES), jnp.int32)
    for r in range(requests):
        tag = jnp.where(row == r, slot_ref[adapter_ref[r]], tag)
    all_ref[:, WIDTH:] = tag.astype(jnp.float32).astype(jnp.bfloat16)


def attend(queries, incoming_pair, cache_key_value, cache_length, request_adapter, adapter_slot):
    requests = queries.shape[0]
    bf16, f32 = jnp.bfloat16, jnp.float32
    ints = (cache_length, request_adapter, adapter_slot)
    inputs = ints + (queries, incoming_pair, cache_key_value)
    return pl.pallas_call(
        attend_kernel,
        out_shape=(
            pltpu.VMEM((requests, GATHER_CUT), bf16),
            pltpu.VMEM((requests, WIDTH + LANES), bf16),
        ),
        in_specs=[HBM] * 6,
        out_specs=(VMEM,) * 2,
        scratch_shapes=[pltpu.SMEM(x.shape, jnp.int32) for x in ints]
        + [
            pltpu.VMEM(queries.shape, bf16),
            pltpu.VMEM(incoming_pair.shape, bf16),
            pltpu.VMEM(cache_key_value.shape, bf16),
            pltpu.VMEM((requests * QUERY_HEADS, HEAD_SIZE), f32),
            pltpu.VMEM((requests * QUERY_HEADS, HEAD_SIZE), f32),
            pltpu.SemaphoreType.DMA((requests + 5,)),
        ],
        compiler_params=pltpu.CompilerParams(vmem_limit_bytes=20 << 20),
        cost_estimate=cost(10**9, 2 * cache_key_value.size),
        name="attend",
    )(*(pltpu.with_memory_space_constraint(x, pltpu.HBM) for x in inputs))


def stage_kernel(down_ref, down_other_ref, up_ref, out_ref, held, sems):
    del up_ref
    ranks = held.shape[1]
    copies = [
        pltpu.make_async_copy(ref, held.at[i], sems.at[i])
        for i, ref in enumerate((down_ref, down_other_ref))
    ]
    for copy in copies:
        copy.start()
    for i, copy in enumerate(copies):
        copy.wait()
        for k in range(0, WIDTH, 1024):
            out_ref[k : k + 1024, i * ranks : (i + 1) * ranks] = held[i, :, k : k + 1024].T


def stage(down, down_other, up):
    ranks = down.shape[0] * down.shape[1]
    pair = [x.reshape(ranks, WIDTH) for x in (down, down_other)]
    return pl.pallas_call(
        stage_kernel,
        out_shape=pltpu.VMEM((WIDTH, 2 * ranks), jnp.bfloat16),
        in_specs=[HBM, HBM, VMEM],
        out_specs=VMEM,
        scratch_shapes=[
            pltpu.VMEM((2, ranks, WIDTH), jnp.bfloat16),
            pltpu.SemaphoreType.DMA((2,)),
        ],
        compiler_params=pltpu.CompilerParams(vmem_limit_bytes=16 << 20),
        cost_estimate=cost(10**8, 8 * ranks * WIDTH),
        name="stage",
    )(*(pltpu.with_memory_space_constraint(x, pltpu.HBM) for x in pair), held_in_vmem(up))


def shrink_kernel(held, rank, device_ref, rows_ref, factors_ref, weight_ref, own_ref, other_ref):
    del weight_ref
    half = rows_ref.shape[0]
    ranks = held * rank
    head = own_ref.shape[1] - ranks
    me = device_ref[0]
    terms = jnp.dot(rows_ref[:, :WIDTH], factors_ref[...], preferred_element_type=jnp.float32)
    slot = rows_ref[:, WIDTH : WIDTH + LANES].astype(jnp.float32)[:, :1]
    column = lax.broadcasted_iota(jnp.int32, (half, ranks), 1)
    for i, (device, ref) in enumerate(((me, own_ref), (me ^ 1, other_ref))):
        owned = (device * held + column // rank).astype(jnp.float32)
        part = terms[:, i * ranks : (i + 1) * ranks]
        shrunk = jnp.where(slot == owned, part, 0.0).astype(jnp.bfloat16)
        ref[:, head:] = shrunk * jnp.bfloat16(ADAPTER_GAIN)
        ref[:, :head] = rows_ref[:, pl.ds(pl.multiple_of(device * head, head), head)]


def shrink(device, rows, factors, up, weight):
    half, head = rows.shape[0], weight.shape[0]
    ranks = up.shape[0] * up.shape[1]
    out = jax.ShapeDtypeStruct((half, head + ranks), jnp.bfloat16)
    return pl.pallas_call(
        functools.partial(shrink_kernel, up.shape[0], up.shape[1]),
        out_shape=(out, out),
        in_specs=[SMEM] + [VMEM] * 3,
        out_specs=(VMEM, VMEM),
        compiler_params=pltpu.CompilerParams(vmem_limit_bytes=16 << 20),
        cost_estimate=cost(4 * half * ranks * WIDTH, 4 * ranks * WIDTH),
        name="shrink",
    )(device, rows, held_in_vmem(factors), held_in_vmem(weight))


def project_kernel(tile, x_ref, x_other_ref, weight_ref, up_ref, own_ref, other_ref):
    half, columns = own_ref.shape
    held, rank, _ = up_ref.shape
    head = weight_ref.shape[0]
    x = jnp.concatenate([x_other_ref[...], x_ref[...]], axis=0)
    for start in range(0, columns, tile):
        at = slice(start, start + tile)
        out = jnp.dot(x[:, :head], weight_ref[:, at], preferred_element_type=jnp.float32)
        out += jnp.dot(
            x[:, head:], up_ref[:, :, at].reshape(held * rank, tile),
            preferred_element_type=jnp.float32,
        )
        other_ref[:, at] = out[:half].astype(jnp.bfloat16)
        own_ref[:, at] = out[half:]


def project(x, x_other, weight, up):
    half, columns = x.shape[0], weight.shape[1]
    return pl.pallas_call(
        functools.partial(project_kernel, 512),
        out_shape=(
            jax.ShapeDtypeStruct((half, columns), jnp.float32),
            jax.ShapeDtypeStruct((half, columns), jnp.bfloat16),
        ),
        in_specs=[VMEM] * 4,
        out_specs=(VMEM, VMEM),
        compiler_params=pltpu.CompilerParams(vmem_limit_bytes=16 << 20),
        cost_estimate=cost(4 * half * x.shape[1] * columns, 2 * x.shape[1] * columns),
        name="project",
    )(x, x_other, held_in_vmem(weight), held_in_vmem(up))


def per_device(
    queries, incoming_pair, cache_key_value, cache_length, out_weight,
    adapter_down, adapter_up, request_adapter, adapter_slot, *, members,
):
    depths = members // 4
    f32, bf16 = jnp.float32, jnp.bfloat16

    def swap(x, mask):
        return lax.ppermute(x, "rep", [(i, i ^ mask) for i in range(members)])

    requests = queries.shape[0]
    a, own = attend(
        queries, incoming_pair, cache_key_value, cache_length, request_adapter, adapter_slot
    )

    down = jnp.swapaxes(adapter_down, 1, 2)
    down_other, a, own = lax.optimization_barrier((swap(down, 1), a, own))
    factors = stage(down, down_other, adapter_up)

    apart = range(depths - 1, 0, -1)
    a_far = jnp.concatenate([swap(a, 4 * d) for d in apart], axis=0)
    side = swap(own, 2)
    b_sides = jnp.concatenate([own[:, GATHER_CUT:], side[:, GATHER_CUT:]], axis=0)
    a_side = swap(a_far, 2)
    b_far, _ = lax.optimization_barrier(([swap(b_sides, 4 * d) for d in apart], a_side))
    b_far = jnp.stack(b_far, axis=0)
    b_far = jnp.swapaxes(b_far.reshape(depths - 1, 2, requests, -1), 0, 1)
    b_far = b_far.reshape(2, (depths - 1) * requests, -1)
    rows = jnp.concatenate(
        [
            own, jnp.concatenate([a_far, b_far[0]], axis=1),
            side, jnp.concatenate([a_side, b_far[1]], axis=1),
        ],
        axis=0,
    )

    device = lax.axis_index("rep").astype(jnp.int32).reshape(1)
    x, x_send = shrink(device, rows, factors, adapter_up, out_weight)
    x_other = swap(x_send, 1)

    mine, send = project(x, x_other, out_weight, adapter_up)
    sums = (mine + swap(send, 1).astype(f32)).reshape(2, depths, requests, WIDTH)
    a_sum, b_sum = sums[..., :SCATTER_CUT], sums[..., SCATTER_CUT:]
    a_part = a_sum[0, 1:] + swap(a_sum[1, 1:].astype(bf16), 2).astype(f32)
    b_send = b_sum.astype(bf16)
    a_send = a_part.astype(bf16)
    b_came = [swap(b_send[:, i], 4 * d) for i, d in enumerate(apart, 1)]
    b_came, _ = lax.optimization_barrier((b_came, a_send))
    b_part = b_sum[:, 0]
    for came in b_came:
        b_part = b_part + came.astype(f32)
    a_out = a_sum[0, 0]
    for i, d in enumerate(apart):
        a_out = a_out + swap(a_send[i], 4 * d).astype(f32)
    side = swap(jnp.concatenate([a_sum[1, 0], b_part[1]], axis=1).astype(bf16), 2)
    return (jnp.concatenate([a_out, b_part[0]], axis=1) + side.astype(f32)).astype(bf16)


def solution(mesh):
    in_specs = (
        P(("groups", "rep"), None),
        P(("groups", "rep"), None, None),
        P(("groups", "rep"), None, None, None),
        P(("groups", "rep")),
        P("rep", None),
        P(("groups", "rep"), None, None),
        P(("groups", "rep"), None, None),
        P(("groups", "rep")),
        P("groups"),
    )
    out_specs = P(("groups", "rep"), None)
    return jax.shard_map(
        functools.partial(per_device, members=mesh.shape["rep"]),
        mesh=mesh, in_specs=in_specs, out_specs=out_specs, check_vma=False,
    )
```

```python
import functools

import jax
import jax.numpy as jnp
from jax import lax
from jax.experimental import pallas as pl
from jax.experimental.pallas import tpu as pltpu
from jax.sharding import PartitionSpec as P

QUERY_HEADS = 64
KEY_VALUE_HEADS = 8
HEAD_SIZE = 128
GROUP = QUERY_HEADS // KEY_VALUE_HEADS
WIDTH = QUERY_HEADS * HEAD_SIZE
LANES = 128
BATCH = 4
ADAPTER_GAIN = 2.0
MASKED_SCORE = -1e30

GATHER_CUT = 5888
SCATTER_CUT = 6144

NT = (((1,), (1,)), ((), ()))
VMEM = pl.BlockSpec(memory_space=pltpu.VMEM)
HBM = pl.BlockSpec(memory_space=pltpu.HBM)
SMEM = pl.BlockSpec(memory_space=pltpu.SMEM)


def held_in_vmem(x):
    return pltpu.with_memory_space_constraint(x, pltpu.VMEM)


def cost(flops, size):
    return pl.CostEstimate(flops=flops, bytes_accessed=size, transcendentals=0)


def per_head(row):
    return jnp.concatenate(
        [
            jnp.broadcast_to(row[:, k * HEAD_SIZE : (k + 1) * HEAD_SIZE], (GROUP, HEAD_SIZE))
            for k in range(KEY_VALUE_HEADS)
        ],
        axis=0,
    )


def attend_kernel(
    length_hbm, adapter_hbm, slot_hbm, query_hbm, pair_hbm, cache_hbm, a_ref, all_ref,
    length_ref, adapter_ref, slot_ref, query_ref, pair_ref, cache, spread, mixed, sems,
):
    requests = query_ref.shape[0]
    slots = cache.shape[2]

    def fetch(r):
        return pltpu.make_async_copy(cache_hbm.at[r], cache.at[r], sems.at[r])

    small = [
        pltpu.make_async_copy(source, target, sems.at[requests + i])
        for i, (source, target) in enumerate(
            (
                (query_hbm, query_ref), (pair_hbm, pair_ref), (length_hbm, length_ref),
                (adapter_hbm, adapter_ref), (slot_hbm, slot_ref),
            )
        )
    ]
    for copy in small:
        copy.start()
    for r in range(requests):
        fetch(r).start()
    for copy in small:
        copy.wait()
    scaling = HEAD_SIZE ** (-0.5)
    for h in range(QUERY_HEADS):
        spread[pl.ds(h, requests, stride=QUERY_HEADS), :] = query_ref[
            :, h * HEAD_SIZE : (h + 1) * HEAD_SIZE
        ].astype(jnp.float32)
    position = lax.broadcasted_iota(jnp.int32, (QUERY_HEADS, slots), 1)
    blank = jnp.zeros((GROUP, HEAD_SIZE), jnp.float32)
    pairs = KEY_VALUE_HEADS // 2
    for r in range(0, requests, BATCH):
        batch = range(r, r + BATCH)
        for t in batch:
            fetch(t).wait()
        scores = []
        for t in batch:
            rows = spread[t * QUERY_HEADS : (t + 1) * QUERY_HEADS, :]
            parts = []
            for j in range(pairs):
                upper = rows[2 * j * GROUP : (2 * j + 1) * GROUP]
                lower = rows[(2 * j + 1) * GROUP : (2 * j + 2) * GROUP]
                both = jnp.concatenate(
                    [
                        jnp.concatenate([upper, blank], axis=1),
                        jnp.concatenate([blank, lower], axis=1),
                    ],
                    axis=0,
                ).astype(jnp.bfloat16)
                keys = cache[t, 0, :, 2 * j * HEAD_SIZE : (2 * j + 2) * HEAD_SIZE]
                parts.append(lax.dot_general(both, keys, NT, preferred_element_type=jnp.float32))
            live = position < length_ref[t]
            score = jnp.concatenate(parts, axis=0) * scaling
            scores.append((rows, live, jnp.where(live, score, MASKED_SCORE)))
        probs = []
        for t, (rows, live, score) in zip(batch, scores):
            new = pair_ref[t].astype(jnp.float32)
            own_score = jnp.sum(rows * per_head(new[0:1]), axis=1, keepdims=True) * scaling
            top = jnp.maximum(jnp.max(score, axis=1, keepdims=True), own_score)
            weight = jnp.where(live, jnp.exp(score - top), 0.0)
            own_weight = jnp.exp(own_score - top)
            total = jnp.sum(weight, axis=1, keepdims=True) + own_weight
            prob = (weight / total).astype(jnp.bfloat16)
            own_prob = (own_weight / total).astype(jnp.bfloat16).astype(jnp.float32)
            probs.append((prob, own_prob * per_head(new[1:2])))
        for t, (prob, own_part) in zip(batch, probs):
            outs = []
            for j in range(pairs):
                values = cache[t, 1, :, 2 * j * HEAD_SIZE : (2 * j + 2) * HEAD_SIZE]
                both = jnp.dot(
                    prob[2 * j * GROUP : (2 * j + 2) * GROUP], values,
                    preferred_element_type=jnp.float32,
                )
                outs += [both[:GROUP, :HEAD_SIZE], both[GROUP:, HEAD_SIZE:]]
            mixed[t * QUERY_HEADS : (t + 1) * QUERY_HEADS, :] = (
                jnp.concatenate(outs, axis=0) + own_part
            )
    for h in range(QUERY_HEADS):
        column = h * HEAD_SIZE
        out = mixed[pl.ds(h, requests, stride=QUERY_HEADS), :].astype(jnp.bfloat16)
        all_ref[:, column : column + HEAD_SIZE] = out
        if column < a_ref.shape[1]:
            a_ref[:, column : column + HEAD_SIZE] = out
    row = lax.broadcasted_iota(jnp.int32, (requests, LANES), 0)
    tag = jnp.zeros((requests, LANES), jnp.int32)
    for r in range(requests):
        tag = jnp.where(row == r, slot_ref[adapter_ref[r]], tag)
    all_ref[:, WIDTH:] = tag.astype(jnp.float32).astype(jnp.bfloat16)


def attend(queries, incoming_pair, cache_key_value, cache_length, request_adapter, adapter_slot):
    requests = queries.shape[0]
    bf16, f32 = jnp.bfloat16, jnp.float32
    ints = (cache_length, request_adapter, adapter_slot)
    inputs = ints + (queries, incoming_pair, cache_key_value)
    return pl.pallas_call(
        attend_kernel,
        out_shape=(
            pltpu.VMEM((requests, GATHER_CUT), bf16),
            pltpu.VMEM((requests, WIDTH + LANES), bf16),
        ),
        in_specs=[HBM] * 6,
        out_specs=(VMEM,) * 2,
        scratch_shapes=[pltpu.SMEM(x.shape, jnp.int32) for x in ints]
        + [
            pltpu.VMEM(queries.shape, bf16),
            pltpu.VMEM(incoming_pair.shape, bf16),
            pltpu.VMEM(cache_key_value.shape, bf16),
            pltpu.VMEM((requests * QUERY_HEADS, HEAD_SIZE), f32),
            pltpu.VMEM((requests * QUERY_HEADS, HEAD_SIZE), f32),
            pltpu.SemaphoreType.DMA((requests + 5,)),
        ],
        compiler_params=pltpu.CompilerParams(vmem_limit_bytes=20 << 20),
        cost_estimate=cost(10**9, 2 * cache_key_value.size),
        name="attend",
    )(*(pltpu.with_memory_space_constraint(x, pltpu.HBM) for x in inputs))


def stage_kernel(down_ref, down_other_ref, up_ref, out_ref, held, sems):
    del up_ref
    ranks = held.shape[1]
    copies = [
        pltpu.make_async_copy(ref, held.at[i], sems.at[i])
        for i, ref in enumerate((down_ref, down_other_ref))
    ]
    for copy in copies:
        copy.start()
    for i, copy in enumerate(copies):
        copy.wait()
        for k in range(0, WIDTH, 1024):
            out_ref[k : k + 1024, i * ranks : (i + 1) * ranks] = held[i, :, k : k + 1024].T


def stage(down, down_other, up):
    ranks = down.shape[0] * down.shape[1]
    pair = [x.reshape(ranks, WIDTH) for x in (down, down_other)]
    return pl.pallas_call(
        stage_kernel,
        out_shape=pltpu.VMEM((WIDTH, 2 * ranks), jnp.bfloat16),
        in_specs=[HBM, HBM, VMEM],
        out_specs=VMEM,
        scratch_shapes=[
            pltpu.VMEM((2, ranks, WIDTH), jnp.bfloat16),
            pltpu.SemaphoreType.DMA((2,)),
        ],
        compiler_params=pltpu.CompilerParams(vmem_limit_bytes=16 << 20),
        cost_estimate=cost(10**8, 8 * ranks * WIDTH),
        name="stage",
    )(*(pltpu.with_memory_space_constraint(x, pltpu.HBM) for x in pair), held_in_vmem(up))


def shrink_kernel(held, rank, device_ref, rows_ref, factors_ref, weight_ref, own_ref, other_ref):
    del weight_ref
    half = rows_ref.shape[0]
    ranks = held * rank
    head = own_ref.shape[1] - ranks
    me = device_ref[0]
    terms = jnp.dot(rows_ref[:, :WIDTH], factors_ref[...], preferred_element_type=jnp.float32)
    slot = rows_ref[:, WIDTH : WIDTH + LANES].astype(jnp.float32)[:, :1]
    column = lax.broadcasted_iota(jnp.int32, (half, ranks), 1)
    for i, (device, ref) in enumerate(((me, own_ref), (me ^ 1, other_ref))):
        owned = (device * held + column // rank).astype(jnp.float32)
        part = terms[:, i * ranks : (i + 1) * ranks]
        shrunk = jnp.where(slot == owned, part, 0.0).astype(jnp.bfloat16)
        ref[:, head:] = shrunk * jnp.bfloat16(ADAPTER_GAIN)
        ref[:, :head] = rows_ref[:, pl.ds(pl.multiple_of(device * head, head), head)]


def shrink(device, rows, factors, up, weight):
    half, head = rows.shape[0], weight.shape[0]
    ranks = up.shape[0] * up.shape[1]
    out = jax.ShapeDtypeStruct((half, head + ranks), jnp.bfloat16)
    return pl.pallas_call(
        functools.partial(shrink_kernel, up.shape[0], up.shape[1]),
        out_shape=(out, out),
        in_specs=[SMEM] + [VMEM] * 3,
        out_specs=(VMEM, VMEM),
        compiler_params=pltpu.CompilerParams(vmem_limit_bytes=16 << 20),
        cost_estimate=cost(4 * half * ranks * WIDTH, 4 * ranks * WIDTH),
        name="shrink",
    )(device, rows, held_in_vmem(factors), held_in_vmem(weight))


def project_kernel(first, tile, x_ref, x_other_ref, weight_ref, up_ref, own_ref, other_ref):
    half, columns = own_ref.shape
    held, rank, _ = up_ref.shape
    head = weight_ref.shape[0]
    x = jnp.concatenate([x_other_ref[...], x_ref[...]], axis=0)
    for start in range(0, columns, tile):
        at = slice(start, min(start + tile, columns))
        there = slice(first + at.start, first + at.stop)
        out = jnp.dot(x[:, :head], weight_ref[:, there], preferred_element_type=jnp.float32)
        out += jnp.dot(
            x[:, head:], up_ref[:, :, there].reshape(held * rank, -1),
            preferred_element_type=jnp.float32,
        )
        other_ref[:, at] = out[:half].astype(jnp.bfloat16)
        own_ref[:, at] = out[half:]


def project(x, x_other, weight, up, first, columns):
    half = x.shape[0]
    return pl.pallas_call(
        functools.partial(project_kernel, first, 512),
        out_shape=(
            jax.ShapeDtypeStruct((half, columns), jnp.float32),
            jax.ShapeDtypeStruct((half, columns), jnp.bfloat16),
        ),
        in_specs=[VMEM] * 4,
        out_specs=(VMEM, VMEM),
        compiler_params=pltpu.CompilerParams(vmem_limit_bytes=16 << 20),
        cost_estimate=cost(4 * half * x.shape[1] * columns, 2 * x.shape[1] * columns),
        name="project",
    )(x, x_other, held_in_vmem(weight), held_in_vmem(up))


def per_device(
    queries, incoming_pair, cache_key_value, cache_length, out_weight,
    adapter_down, adapter_up, request_adapter, adapter_slot, *, members,
):
    depths = members // 4
    f32, bf16 = jnp.float32, jnp.bfloat16

    def swap(x, mask):
        return lax.ppermute(x, "rep", [(i, i ^ mask) for i in range(members)])

    requests = queries.shape[0]
    a, own = attend(
        queries, incoming_pair, cache_key_value, cache_length, request_adapter, adapter_slot
    )

    down = jnp.swapaxes(adapter_down, 1, 2)
    down_other, a, own = lax.optimization_barrier((swap(down, 1), a, own))
    factors = stage(down, down_other, adapter_up)

    apart = range(depths - 1, 0, -1)
    a_far = jnp.concatenate([swap(a, 4 * d) for d in apart], axis=0)
    side = swap(own, 2)
    b_sides = jnp.concatenate([own[:, GATHER_CUT:], side[:, GATHER_CUT:]], axis=0)
    a_side = swap(a_far, 2)
    b_far, _ = lax.optimization_barrier(([swap(b_sides, 4 * d) for d in apart], a_side))
    b_far = jnp.stack(b_far, axis=0)
    b_far = jnp.swapaxes(b_far.reshape(depths - 1, 2, requests, -1), 0, 1)
    b_far = b_far.reshape(2, (depths - 1) * requests, -1)
    rows = jnp.concatenate(
        [
            own, jnp.concatenate([a_far, b_far[0]], axis=1),
            side, jnp.concatenate([a_side, b_far[1]], axis=1),
        ],
        axis=0,
    )

    device = lax.axis_index("rep").astype(jnp.int32).reshape(1)
    x, x_send = shrink(device, rows, factors, adapter_up, out_weight)
    x_other = swap(x_send, 1)

    def sums(mine, came):
        return (mine + came.astype(f32)).reshape(2, depths, requests, -1)

    mine, send = project(x, x_other, out_weight, adapter_up, 0, SCATTER_CUT)
    came = swap(send, 1)
    a_sum = sums(mine, came)
    x, came = lax.optimization_barrier((x, came))
    mine, send = project(x, x_other, out_weight, adapter_up, SCATTER_CUT, WIDTH - SCATTER_CUT)
    b_sum = sums(mine, swap(send, 1))
    a_part = a_sum[0, 1:] + swap(a_sum[1, 1:].astype(bf16), 2).astype(f32)
    b_send = b_sum.astype(bf16)
    a_send = a_part.astype(bf16)
    b_came = [swap(b_send[:, i], 4 * d) for i, d in enumerate(apart, 1)]
    b_came, _ = lax.optimization_barrier((b_came, a_send))
    b_part = b_sum[:, 0]
    for came in b_came:
        b_part = b_part + came.astype(f32)
    a_out = a_sum[0, 0]
    for i, d in enumerate(apart):
        a_out = a_out + swap(a_send[i], 4 * d).astype(f32)
    side = swap(jnp.concatenate([a_sum[1, 0], b_part[1]], axis=1).astype(bf16), 2)
    return (jnp.concatenate([a_out, b_part[0]], axis=1) + side.astype(f32)).astype(bf16)


def solution(mesh):
    in_specs = (
        P(("groups", "rep"), None),
        P(("groups", "rep"), None, None),
        P(("groups", "rep"), None, None, None),
        P(("groups", "rep")),
        P("rep", None),
        P(("groups", "rep"), None, None),
        P(("groups", "rep"), None, None),
        P(("groups", "rep")),
        P("groups"),
    )
    out_specs = P(("groups", "rep"), None)
    return jax.shard_map(
        functools.partial(per_device, members=mesh.shape["rep"]),
        mesh=mesh, in_specs=in_specs, out_specs=out_specs, check_vma=False,
    )
```

```python
import functools

import jax
import jax.numpy as jnp
from jax import lax
from jax.experimental import pallas as pl
from jax.experimental.pallas import tpu as pltpu
from jax.sharding import PartitionSpec as P

QUERY_HEADS = 64
KEY_VALUE_HEADS = 8
HEAD_SIZE = 128
GROUP = QUERY_HEADS // KEY_VALUE_HEADS
WIDTH = QUERY_HEADS * HEAD_SIZE
LANES = 128
BATCH = 4
ADAPTER_GAIN = 2.0
MASKED_SCORE = -1e30

GATHER_CUT = 5888
SCATTER_CUT = 6144

NT = (((1,), (1,)), ((), ()))
VMEM = pl.BlockSpec(memory_space=pltpu.VMEM)
HBM = pl.BlockSpec(memory_space=pltpu.HBM)
SMEM = pl.BlockSpec(memory_space=pltpu.SMEM)


def held_in_vmem(x):
    return pltpu.with_memory_space_constraint(x, pltpu.VMEM)


def cost(flops, size):
    return pl.CostEstimate(flops=flops, bytes_accessed=size, transcendentals=0)


def per_head(row):
    return jnp.concatenate(
        [
            jnp.broadcast_to(row[:, k * HEAD_SIZE : (k + 1) * HEAD_SIZE], (GROUP, HEAD_SIZE))
            for k in range(KEY_VALUE_HEADS)
        ],
        axis=0,
    )


def attend_kernel(
    length_hbm, adapter_hbm, slot_hbm, query_hbm, pair_hbm, cache_hbm, a_ref, all_ref,
    length_ref, adapter_ref, slot_ref, query_ref, pair_ref, cache, spread, mixed, sems,
):
    requests = query_ref.shape[0]
    slots = cache.shape[2]

    def fetch(r):
        return pltpu.make_async_copy(cache_hbm.at[r], cache.at[r], sems.at[r])

    small = [
        pltpu.make_async_copy(source, target, sems.at[requests + i])
        for i, (source, target) in enumerate(
            (
                (query_hbm, query_ref), (pair_hbm, pair_ref), (length_hbm, length_ref),
                (adapter_hbm, adapter_ref), (slot_hbm, slot_ref),
            )
        )
    ]
    for copy in small:
        copy.start()
    for r in range(requests):
        fetch(r).start()
    for copy in small:
        copy.wait()
    scaling = HEAD_SIZE ** (-0.5)
    for h in range(QUERY_HEADS):
        spread[pl.ds(h, requests, stride=QUERY_HEADS), :] = query_ref[
            :, h * HEAD_SIZE : (h + 1) * HEAD_SIZE
        ].astype(jnp.float32)
    position = lax.broadcasted_iota(jnp.int32, (QUERY_HEADS, slots), 1)
    blank = jnp.zeros((GROUP, HEAD_SIZE), jnp.float32)
    pairs = KEY_VALUE_HEADS // 2
    for r in range(0, requests, BATCH):
        batch = range(r, r + BATCH)
        for t in batch:
            fetch(t).wait()
        scores = []
        for t in batch:
            rows = spread[t * QUERY_HEADS : (t + 1) * QUERY_HEADS, :]
            parts = []
            for j in range(pairs):
                upper = rows[2 * j * GROUP : (2 * j + 1) * GROUP]
                lower = rows[(2 * j + 1) * GROUP : (2 * j + 2) * GROUP]
                both = jnp.concatenate(
                    [
                        jnp.concatenate([upper, blank], axis=1),
                        jnp.concatenate([blank, lower], axis=1),
                    ],
                    axis=0,
                ).astype(jnp.bfloat16)
                keys = cache[t, 0, :, 2 * j * HEAD_SIZE : (2 * j + 2) * HEAD_SIZE]
                parts.append(lax.dot_general(both, keys, NT, preferred_element_type=jnp.float32))
            live = position < length_ref[t]
            score = jnp.concatenate(parts, axis=0) * scaling
            scores.append((rows, live, jnp.where(live, score, MASKED_SCORE)))
        probs = []
        for t, (rows, live, score) in zip(batch, scores):
            new = pair_ref[t].astype(jnp.float32)
            own_score = jnp.sum(rows * per_head(new[0:1]), axis=1, keepdims=True) * scaling
            top = jnp.maximum(jnp.max(score, axis=1, keepdims=True), own_score)
            weight = jnp.where(live, jnp.exp(score - top), 0.0)
            own_weight = jnp.exp(own_score - top)
            total = jnp.sum(weight, axis=1, keepdims=True) + own_weight
            prob = (weight / total).astype(jnp.bfloat16)
            own_prob = (own_weight / total).astype(jnp.bfloat16).astype(jnp.float32)
            probs.append((prob, own_prob * per_head(new[1:2])))
        for t, (prob, own_part) in zip(batch, probs):
            outs = []
            for j in range(pairs):
                values = cache[t, 1, :, 2 * j * HEAD_SIZE : (2 * j + 2) * HEAD_SIZE]
                both = jnp.dot(
                    prob[2 * j * GROUP : (2 * j + 2) * GROUP], values,
                    preferred_element_type=jnp.float32,
                )
                outs += [both[:GROUP, :HEAD_SIZE], both[GROUP:, HEAD_SIZE:]]
            mixed[t * QUERY_HEADS : (t + 1) * QUERY_HEADS, :] = (
                jnp.concatenate(outs, axis=0) + own_part
            )
    for h in range(QUERY_HEADS):
        column = h * HEAD_SIZE
        out = mixed[pl.ds(h, requests, stride=QUERY_HEADS), :].astype(jnp.bfloat16)
        all_ref[:, column : column + HEAD_SIZE] = out
        if column < a_ref.shape[1]:
            a_ref[:, column : column + HEAD_SIZE] = out
    row = lax.broadcasted_iota(jnp.int32, (requests, LANES), 0)
    tag = jnp.zeros((requests, LANES), jnp.int32)
    for r in range(requests):
        tag = jnp.where(row == r, slot_ref[adapter_ref[r]], tag)
    all_ref[:, WIDTH:] = tag.astype(jnp.float32).astype(jnp.bfloat16)


def attend(queries, incoming_pair, cache_key_value, cache_length, request_adapter, adapter_slot):
    requests = queries.shape[0]
    bf16, f32 = jnp.bfloat16, jnp.float32
    ints = (cache_length, request_adapter, adapter_slot)
    inputs = ints + (queries, incoming_pair, cache_key_value)
    return pl.pallas_call(
        attend_kernel,
        out_shape=(
            pltpu.VMEM((requests, GATHER_CUT), bf16),
            pltpu.VMEM((requests, WIDTH + LANES), bf16),
        ),
        in_specs=[HBM] * 6,
        out_specs=(VMEM,) * 2,
        scratch_shapes=[pltpu.SMEM(x.shape, jnp.int32) for x in ints]
        + [
            pltpu.VMEM(queries.shape, bf16),
            pltpu.VMEM(incoming_pair.shape, bf16),
            pltpu.VMEM(cache_key_value.shape, bf16),
            pltpu.VMEM((requests * QUERY_HEADS, HEAD_SIZE), f32),
            pltpu.VMEM((requests * QUERY_HEADS, HEAD_SIZE), f32),
            pltpu.SemaphoreType.DMA((requests + 5,)),
        ],
        compiler_params=pltpu.CompilerParams(vmem_limit_bytes=20 << 20),
        cost_estimate=cost(10**9, 2 * cache_key_value.size),
        name="attend",
    )(*(pltpu.with_memory_space_constraint(x, pltpu.HBM) for x in inputs))


def stage_kernel(down_ref, down_other_ref, up_ref, out_ref, held, sems):
    del up_ref
    ranks = held.shape[1]
    copies = [
        pltpu.make_async_copy(ref, held.at[i], sems.at[i])
        for i, ref in enumerate((down_ref, down_other_ref))
    ]
    for copy in copies:
        copy.start()
    for i, copy in enumerate(copies):
        copy.wait()
        for k in range(0, WIDTH, 1024):
            out_ref[k : k + 1024, i * ranks : (i + 1) * ranks] = held[i, :, k : k + 1024].T


def stage(down, down_other, up):
    ranks = down.shape[0] * down.shape[1]
    pair = [x.reshape(ranks, WIDTH) for x in (down, down_other)]
    return pl.pallas_call(
        stage_kernel,
        out_shape=pltpu.VMEM((WIDTH, 2 * ranks), jnp.bfloat16),
        in_specs=[HBM, HBM, VMEM],
        out_specs=VMEM,
        scratch_shapes=[
            pltpu.VMEM((2, ranks, WIDTH), jnp.bfloat16),
            pltpu.SemaphoreType.DMA((2,)),
        ],
        compiler_params=pltpu.CompilerParams(vmem_limit_bytes=16 << 20),
        cost_estimate=cost(10**8, 8 * ranks * WIDTH),
        name="stage",
    )(*(pltpu.with_memory_space_constraint(x, pltpu.HBM) for x in pair), held_in_vmem(up))


def shrink_kernel(held, rank, device_ref, rows_ref, factors_ref, weight_ref, own_ref, other_ref):
    del weight_ref
    half = rows_ref.shape[0]
    ranks = held * rank
    head = own_ref.shape[1] - ranks
    me = device_ref[0]
    terms = jnp.dot(rows_ref[:, :WIDTH], factors_ref[...], preferred_element_type=jnp.float32)
    slot = rows_ref[:, WIDTH : WIDTH + LANES].astype(jnp.float32)[:, :1]
    column = lax.broadcasted_iota(jnp.int32, (half, ranks), 1)
    for i, (device, ref) in enumerate(((me, own_ref), (me ^ 1, other_ref))):
        owned = (device * held + column // rank).astype(jnp.float32)
        part = terms[:, i * ranks : (i + 1) * ranks]
        shrunk = jnp.where(slot == owned, part, 0.0).astype(jnp.bfloat16)
        ref[:, head:] = shrunk * jnp.bfloat16(ADAPTER_GAIN)
        ref[:, :head] = rows_ref[:, pl.ds(pl.multiple_of(device * head, head), head)]


def shrink(device, rows, factors, up, weight):
    half, head = rows.shape[0], weight.shape[0]
    ranks = up.shape[0] * up.shape[1]
    out = jax.ShapeDtypeStruct((half, head + ranks), jnp.bfloat16)
    return pl.pallas_call(
        functools.partial(shrink_kernel, up.shape[0], up.shape[1]),
        out_shape=(out, out),
        in_specs=[SMEM] + [VMEM] * 3,
        out_specs=(VMEM, VMEM),
        compiler_params=pltpu.CompilerParams(vmem_limit_bytes=16 << 20),
        cost_estimate=cost(4 * half * ranks * WIDTH, 4 * ranks * WIDTH),
        name="shrink",
    )(device, rows, held_in_vmem(factors), held_in_vmem(weight))


def project_kernel(first, tile, x_ref, x_other_ref, weight_ref, up_ref, own_ref, other_ref):
    half, columns = own_ref.shape
    held, rank, _ = up_ref.shape
    head = weight_ref.shape[0]
    x = jnp.concatenate([x_other_ref[...], x_ref[...]], axis=0)
    for start in range(0, columns, tile):
        at = slice(start, min(start + tile, columns))
        there = slice(first + at.start, first + at.stop)
        out = jnp.dot(x[:, :head], weight_ref[:, there], preferred_element_type=jnp.float32)
        out += jnp.dot(
            x[:, head:], up_ref[:, :, there].reshape(held * rank, -1),
            preferred_element_type=jnp.float32,
        )
        other_ref[:, at] = out[:half].astype(jnp.bfloat16)
        own_ref[:, at] = out[half:]


def project(x, x_other, weight, up, first, columns):
    half = x.shape[0]
    return pl.pallas_call(
        functools.partial(project_kernel, first, 512),
        out_shape=(
            jax.ShapeDtypeStruct((half, columns), jnp.float32),
            jax.ShapeDtypeStruct((half, columns), jnp.bfloat16),
        ),
        in_specs=[VMEM] * 4,
        out_specs=(VMEM, VMEM),
        compiler_params=pltpu.CompilerParams(vmem_limit_bytes=16 << 20),
        cost_estimate=cost(4 * half * x.shape[1] * columns, 2 * x.shape[1] * columns),
        name="project",
    )(x, x_other, held_in_vmem(weight), held_in_vmem(up))


def per_device(
    queries, incoming_pair, cache_key_value, cache_length, out_weight,
    adapter_down, adapter_up, request_adapter, adapter_slot, *, members,
):
    depths = members // 4
    f32, bf16 = jnp.float32, jnp.bfloat16

    def swap(x, mask):
        return lax.ppermute(x, "rep", [(i, i ^ mask) for i in range(members)])

    requests = queries.shape[0]
    a, own = attend(
        queries, incoming_pair, cache_key_value, cache_length, request_adapter, adapter_slot
    )

    apart = range(depths - 1, 0, -1)
    a_far = jnp.concatenate([swap(a, 4 * d) for d in apart], axis=0)
    side = swap(own, 2)
    down = jnp.swapaxes(adapter_down, 1, 2)
    down_other, a_far, side = lax.optimization_barrier((swap(down, 1), a_far, side))
    factors = stage(down, down_other, adapter_up)
    b_sides = jnp.concatenate([own[:, GATHER_CUT:], side[:, GATHER_CUT:]], axis=0)
    a_side = swap(a_far, 2)
    b_far, _ = lax.optimization_barrier(([swap(b_sides, 4 * d) for d in apart], a_side))
    b_far = jnp.stack(b_far, axis=0)
    b_far = jnp.swapaxes(b_far.reshape(depths - 1, 2, requests, -1), 0, 1)
    b_far = b_far.reshape(2, (depths - 1) * requests, -1)
    rows = jnp.concatenate(
        [
            own, jnp.concatenate([a_far, b_far[0]], axis=1),
            side, jnp.concatenate([a_side, b_far[1]], axis=1),
        ],
        axis=0,
    )

    device = lax.axis_index("rep").astype(jnp.int32).reshape(1)
    x, x_send = shrink(device, rows, factors, adapter_up, out_weight)
    x_other = swap(x_send, 1)

    def sums(mine, came):
        return (mine + came.astype(f32)).reshape(2, depths, requests, -1)

    mine, send = project(x, x_other, out_weight, adapter_up, 0, SCATTER_CUT)
    came = swap(send, 1)
    a_sum = sums(mine, came)
    x, came = lax.optimization_barrier((x, came))
    mine, send = project(x, x_other, out_weight, adapter_up, SCATTER_CUT, WIDTH - SCATTER_CUT)
    b_sum = sums(mine, swap(send, 1))
    a_part = a_sum[0, 1:] + swap(a_sum[1, 1:].astype(bf16), 2).astype(f32)
    b_send = b_sum.astype(bf16)
    a_send = a_part.astype(bf16)
    b_came = [swap(b_send[:, i], 4 * d) for i, d in enumerate(apart, 1)]
    b_came, _ = lax.optimization_barrier((b_came, a_send))
    b_part = b_sum[:, 0]
    for came in b_came:
        b_part = b_part + came.astype(f32)
    a_out = a_sum[0, 0]
    for i, d in enumerate(apart):
        a_out = a_out + swap(a_send[i], 4 * d).astype(f32)
    side = swap(jnp.concatenate([a_sum[1, 0], b_part[1]], axis=1).astype(bf16), 2)
    return (jnp.concatenate([a_out, b_part[0]], axis=1) + side.astype(f32)).astype(bf16)


def solution(mesh):
    in_specs = (
        P(("groups", "rep"), None),
        P(("groups", "rep"), None, None),
        P(("groups", "rep"), None, None, None),
        P(("groups", "rep")),
        P("rep", None),
        P(("groups", "rep"), None, None),
        P(("groups", "rep"), None, None),
        P(("groups", "rep")),
        P("groups"),
    )
    out_specs = P(("groups", "rep"), None)
    return jax.shard_map(
        functools.partial(per_device, members=mesh.shape["rep"]),
        mesh=mesh, in_specs=in_specs, out_specs=out_specs, check_vma=False,
    )
```

```python
import functools

import jax
import jax.numpy as jnp
from jax import lax
from jax.experimental import pallas as pl
from jax.experimental.pallas import tpu as pltpu
from jax.sharding import PartitionSpec as P

QUERY_HEADS = 64
KEY_VALUE_HEADS = 8
HEAD_SIZE = 128
GROUP = QUERY_HEADS // KEY_VALUE_HEADS
WIDTH = QUERY_HEADS * HEAD_SIZE
LANES = 128
FIRST = 3
ADAPTER_GAIN = 2.0
MASKED_SCORE = -1e30

GATHER_CUT = 6144
SCATTER_CUT = 6144

NT = (((1,), (1,)), ((), ()))
VMEM = pl.BlockSpec(memory_space=pltpu.VMEM)
HBM = pl.BlockSpec(memory_space=pltpu.HBM)
SMEM = pl.BlockSpec(memory_space=pltpu.SMEM)


def held_in_vmem(x):
    return pltpu.with_memory_space_constraint(x, pltpu.VMEM)


def cost(flops, size):
    return pl.CostEstimate(flops=flops, bytes_accessed=size, transcendentals=0)


def per_head(row):
    return jnp.concatenate(
        [
            jnp.broadcast_to(row[:, k * HEAD_SIZE : (k + 1) * HEAD_SIZE], (GROUP, HEAD_SIZE))
            for k in range(KEY_VALUE_HEADS)
        ],
        axis=0,
    )


def attend_kernel(
    length_hbm, adapter_hbm, slot_hbm, query_hbm, pair_hbm, cache_hbm, a_ref, all_ref,
    length_ref, adapter_ref, slot_ref, query_ref, pair_ref, cache, spread, mixed, sems,
):
    requests = query_ref.shape[0]
    slots = cache.shape[2]

    def fetch(r):
        return pltpu.make_async_copy(cache_hbm.at[r], cache.at[r], sems.at[r])

    small = [
        pltpu.make_async_copy(source, target, sems.at[requests + i])
        for i, (source, target) in enumerate(
            (
                (query_hbm, query_ref), (pair_hbm, pair_ref), (length_hbm, length_ref),
                (adapter_hbm, adapter_ref), (slot_hbm, slot_ref),
            )
        )
    ]
    for copy in small:
        copy.start()
    for r in range(requests):
        fetch(r).start()
    for copy in small:
        copy.wait()
    scaling = HEAD_SIZE ** (-0.5)
    for h in range(QUERY_HEADS):
        spread[pl.ds(h, requests, stride=QUERY_HEADS), :] = query_ref[
            :, h * HEAD_SIZE : (h + 1) * HEAD_SIZE
        ].astype(jnp.float32)
    position = lax.broadcasted_iota(jnp.int32, (QUERY_HEADS, slots), 1)
    blank = jnp.zeros((GROUP, HEAD_SIZE), jnp.float32)
    pairs = KEY_VALUE_HEADS // 2
    for batch in (range(FIRST), range(FIRST, requests)):
        for t in batch:
            fetch(t).wait()
        scores = []
        for t in batch:
            rows = spread[t * QUERY_HEADS : (t + 1) * QUERY_HEADS, :]
            parts = []
            for j in range(pairs):
                upper = rows[2 * j * GROUP : (2 * j + 1) * GROUP]
                lower = rows[(2 * j + 1) * GROUP : (2 * j + 2) * GROUP]
                both = jnp.concatenate(
                    [
                        jnp.concatenate([upper, blank], axis=1),
                        jnp.concatenate([blank, lower], axis=1),
                    ],
                    axis=0,
                ).astype(jnp.bfloat16)
                keys = cache[t, 0, :, 2 * j * HEAD_SIZE : (2 * j + 2) * HEAD_SIZE]
                parts.append(lax.dot_general(both, keys, NT, preferred_element_type=jnp.float32))
            live = position < length_ref[t]
            score = jnp.concatenate(parts, axis=0) * scaling
            scores.append((rows, live, jnp.where(live, score, MASKED_SCORE)))
        probs = []
        for t, (rows, live, score) in zip(batch, scores):
            new = pair_ref[t].astype(jnp.float32)
            own_score = jnp.sum(rows * per_head(new[0:1]), axis=1, keepdims=True) * scaling
            top = jnp.maximum(jnp.max(score, axis=1, keepdims=True), own_score)
            weight = jnp.where(live, jnp.exp(score - top), 0.0)
            own_weight = jnp.exp(own_score - top)
            total = jnp.sum(weight, axis=1, keepdims=True) + own_weight
            prob = (weight / total).astype(jnp.bfloat16)
            own_prob = (own_weight / total).astype(jnp.bfloat16).astype(jnp.float32)
            probs.append((prob, own_prob * per_head(new[1:2])))
        for t, (prob, own_part) in zip(batch, probs):
            outs = []
            for j in range(pairs):
                values = cache[t, 1, :, 2 * j * HEAD_SIZE : (2 * j + 2) * HEAD_SIZE]
                both = jnp.dot(
                    prob[2 * j * GROUP : (2 * j + 2) * GROUP], values,
                    preferred_element_type=jnp.float32,
                )
                outs += [both[:GROUP, :HEAD_SIZE], both[GROUP:, HEAD_SIZE:]]
            mixed[t * QUERY_HEADS : (t + 1) * QUERY_HEADS, :] = (
                jnp.concatenate(outs, axis=0) + own_part
            )
    for h in range(QUERY_HEADS):
        column = h * HEAD_SIZE
        out = mixed[pl.ds(h, requests, stride=QUERY_HEADS), :].astype(jnp.bfloat16)
        all_ref[:, column : column + HEAD_SIZE] = out
        if column < a_ref.shape[1]:
            a_ref[:, column : column + HEAD_SIZE] = out
    row = lax.broadcasted_iota(jnp.int32, (requests, LANES), 0)
    tag = jnp.zeros((requests, LANES), jnp.int32)
    for r in range(requests):
        tag = jnp.where(row == r, slot_ref[adapter_ref[r]], tag)
    all_ref[:, WIDTH:] = tag.astype(jnp.float32).astype(jnp.bfloat16)


def attend(queries, incoming_pair, cache_key_value, cache_length, request_adapter, adapter_slot):
    requests = queries.shape[0]
    bf16, f32 = jnp.bfloat16, jnp.float32
    ints = (cache_length, request_adapter, adapter_slot)
    inputs = ints + (queries, incoming_pair, cache_key_value)
    return pl.pallas_call(
        attend_kernel,
        out_shape=(
            pltpu.VMEM((requests, GATHER_CUT), bf16),
            pltpu.VMEM((requests, WIDTH + LANES), bf16),
        ),
        in_specs=[HBM] * 6,
        out_specs=(VMEM,) * 2,
        scratch_shapes=[pltpu.SMEM(x.shape, jnp.int32) for x in ints]
        + [
            pltpu.VMEM(queries.shape, bf16),
            pltpu.VMEM(incoming_pair.shape, bf16),
            pltpu.VMEM(cache_key_value.shape, bf16),
            pltpu.VMEM((requests * QUERY_HEADS, HEAD_SIZE), f32),
            pltpu.VMEM((requests * QUERY_HEADS, HEAD_SIZE), f32),
            pltpu.SemaphoreType.DMA((requests + 5,)),
        ],
        compiler_params=pltpu.CompilerParams(vmem_limit_bytes=20 << 20),
        cost_estimate=cost(10**9, 2 * cache_key_value.size),
        name="attend",
    )(*(pltpu.with_memory_space_constraint(x, pltpu.HBM) for x in inputs))


def stage_kernel(down_ref, down_other_ref, up_ref, out_ref, held, sems):
    del up_ref
    ranks = held.shape[1]
    copies = [
        pltpu.make_async_copy(ref, held.at[i], sems.at[i])
        for i, ref in enumerate((down_ref, down_other_ref))
    ]
    for copy in copies:
        copy.start()
    for i, copy in enumerate(copies):
        copy.wait()
        for k in range(0, WIDTH, 1024):
            out_ref[k : k + 1024, i * ranks : (i + 1) * ranks] = held[i, :, k : k + 1024].T


def stage(down, down_other, up):
    ranks = down.shape[0] * down.shape[1]
    pair = [x.reshape(ranks, WIDTH) for x in (down, down_other)]
    return pl.pallas_call(
        stage_kernel,
        out_shape=pltpu.VMEM((WIDTH, 2 * ranks), jnp.bfloat16),
        in_specs=[HBM, HBM, VMEM],
        out_specs=VMEM,
        scratch_shapes=[
            pltpu.VMEM((2, ranks, WIDTH), jnp.bfloat16),
            pltpu.SemaphoreType.DMA((2,)),
        ],
        compiler_params=pltpu.CompilerParams(vmem_limit_bytes=16 << 20),
        cost_estimate=cost(10**8, 8 * ranks * WIDTH),
        name="stage",
    )(*(pltpu.with_memory_space_constraint(x, pltpu.HBM) for x in pair), held_in_vmem(up))


def shrink_kernel(held, rank, device_ref, rows_ref, factors_ref, weight_ref, own_ref, other_ref):
    del weight_ref
    half = rows_ref.shape[0]
    ranks = held * rank
    head = own_ref.shape[1] - ranks
    me = device_ref[0]
    terms = jnp.dot(rows_ref[:, :WIDTH], factors_ref[...], preferred_element_type=jnp.float32)
    slot = rows_ref[:, WIDTH : WIDTH + LANES].astype(jnp.float32)[:, :1]
    column = lax.broadcasted_iota(jnp.int32, (half, ranks), 1)
    for i, (device, ref) in enumerate(((me, own_ref), (me ^ 1, other_ref))):
        owned = (device * held + column // rank).astype(jnp.float32)
        part = terms[:, i * ranks : (i + 1) * ranks]
        shrunk = jnp.where(slot == owned, part, 0.0).astype(jnp.bfloat16)
        ref[:, head:] = shrunk * jnp.bfloat16(ADAPTER_GAIN)
        ref[:, :head] = rows_ref[:, pl.ds(pl.multiple_of(device * head, head), head)]


def shrink(device, rows, factors, up, weight):
    half, head = rows.shape[0], weight.shape[0]
    ranks = up.shape[0] * up.shape[1]
    out = jax.ShapeDtypeStruct((half, head + ranks), jnp.bfloat16)
    return pl.pallas_call(
        functools.partial(shrink_kernel, up.shape[0], up.shape[1]),
        out_shape=(out, out),
        in_specs=[SMEM] + [VMEM] * 3,
        out_specs=(VMEM, VMEM),
        compiler_params=pltpu.CompilerParams(vmem_limit_bytes=16 << 20),
        cost_estimate=cost(4 * half * ranks * WIDTH, 4 * ranks * WIDTH),
        name="shrink",
    )(device, rows, held_in_vmem(factors), held_in_vmem(weight))


def project_kernel(first, tile, x_ref, x_other_ref, weight_ref, up_ref, own_ref, other_ref):
    half, columns = own_ref.shape
    held, rank, _ = up_ref.shape
    head = weight_ref.shape[0]
    x = jnp.concatenate([x_other_ref[...], x_ref[...]], axis=0)
    for start in range(0, columns, tile):
        at = slice(start, min(start + tile, columns))
        there = slice(first + at.start, first + at.stop)
        out = jnp.dot(x[:, :head], weight_ref[:, there], preferred_element_type=jnp.float32)
        out += jnp.dot(
            x[:, head:], up_ref[:, :, there].reshape(held * rank, -1),
            preferred_element_type=jnp.float32,
        )
        other_ref[:, at] = out[:half].astype(jnp.bfloat16)
        own_ref[:, at] = out[half:]


def project(x, x_other, weight, up, first, columns):
    half = x.shape[0]
    return pl.pallas_call(
        functools.partial(project_kernel, first, 512),
        out_shape=(
            jax.ShapeDtypeStruct((half, columns), jnp.float32),
            jax.ShapeDtypeStruct((half, columns), jnp.bfloat16),
        ),
        in_specs=[VMEM] * 4,
        out_specs=(VMEM, VMEM),
        compiler_params=pltpu.CompilerParams(vmem_limit_bytes=16 << 20),
        cost_estimate=cost(4 * half * x.shape[1] * columns, 2 * x.shape[1] * columns),
        name="project",
    )(x, x_other, held_in_vmem(weight), held_in_vmem(up))


def per_device(
    queries, incoming_pair, cache_key_value, cache_length, out_weight,
    adapter_down, adapter_up, request_adapter, adapter_slot, *, members,
):
    depths = members // 4
    f32, bf16 = jnp.float32, jnp.bfloat16

    def swap(x, mask):
        return lax.ppermute(x, "rep", [(i, i ^ mask) for i in range(members)])

    requests = queries.shape[0]
    a, own = attend(
        queries, incoming_pair, cache_key_value, cache_length, request_adapter, adapter_slot
    )

    apart = range(depths - 1, 0, -1)
    a_far = jnp.concatenate([swap(a, 4 * d) for d in apart], axis=0)
    side = swap(own, 2)
    down = jnp.swapaxes(adapter_down, 1, 2)
    down_other, a_far, side = lax.optimization_barrier((swap(down, 1), a_far, side))
    factors = stage(down, down_other, adapter_up)
    b_sides = jnp.concatenate([own[:, GATHER_CUT:], side[:, GATHER_CUT:]], axis=0)
    a_side = swap(a_far, 2)
    b_far, _ = lax.optimization_barrier(([swap(b_sides, 4 * d) for d in apart], a_side))
    b_far = jnp.stack(b_far, axis=0)
    b_far = jnp.swapaxes(b_far.reshape(depths - 1, 2, requests, -1), 0, 1)
    b_far = b_far.reshape(2, (depths - 1) * requests, -1)
    rows = jnp.concatenate(
        [
            own, jnp.concatenate([a_far, b_far[0]], axis=1),
            side, jnp.concatenate([a_side, b_far[1]], axis=1),
        ],
        axis=0,
    )

    device = lax.axis_index("rep").astype(jnp.int32).reshape(1)
    x, x_send = shrink(device, rows, factors, adapter_up, out_weight)
    x_other = swap(x_send, 1)

    def sums(mine, came):
        return (mine + came.astype(f32)).reshape(2, depths, requests, -1)

    mine, send = project(x, x_other, out_weight, adapter_up, 0, SCATTER_CUT)
    came = swap(send, 1)
    a_sum = sums(mine, came)
    x, came = lax.optimization_barrier((x, came))
    mine, send = project(x, x_other, out_weight, adapter_up, SCATTER_CUT, WIDTH - SCATTER_CUT)
    b_sum = sums(mine, swap(send, 1))
    a_part = a_sum[0, 1:] + swap(a_sum[1, 1:].astype(bf16), 2).astype(f32)
    b_send = b_sum.astype(bf16)
    a_send = a_part.astype(bf16)
    b_came = [swap(b_send[:, i], 4 * d) for i, d in enumerate(apart, 1)]
    b_came, _ = lax.optimization_barrier((b_came, a_send))
    b_part = b_sum[:, 0]
    for came in b_came:
        b_part = b_part + came.astype(f32)
    a_out = a_sum[0, 0]
    for i, d in enumerate(apart):
        a_out = a_out + swap(a_send[i], 4 * d).astype(f32)
    side = swap(jnp.concatenate([a_sum[1, 0], b_part[1]], axis=1).astype(bf16), 2)
    return (jnp.concatenate([a_out, b_part[0]], axis=1) + side.astype(f32)).astype(bf16)


def solution(mesh):
    in_specs = (
        P(("groups", "rep"), None),
        P(("groups", "rep"), None, None),
        P(("groups", "rep"), None, None, None),
        P(("groups", "rep")),
        P("rep", None),
        P(("groups", "rep"), None, None),
        P(("groups", "rep"), None, None),
        P(("groups", "rep")),
        P("groups"),
    )
    out_specs = P(("groups", "rep"), None)
    return jax.shard_map(
        functools.partial(per_device, members=mesh.shape["rep"]),
        mesh=mesh, in_specs=in_specs, out_specs=out_specs, check_vma=False,
    )
```
